32 devices in a mesh: sec: 2 (over core), grp: 4 (over y, x), tp: 4 (over z).
Axes of the slice: x: 2, y: 2, z: 4, core: 2. Of those that a mesh axis runs over, the one named last changes fastest.
Arguments:
- resid_in: bfloat16 [192, 6144], P(('sec', 'grp'), 'tp'), may hold values from -6 to 6
- queries: bfloat16 [192, 6144], P(('sec', 'grp'), 'tp'), may hold values from -20 to 20
- new_kv: bfloat16 [192, 2, 1024], P(('sec', 'grp'), None, 'tp'), may hold values from -6 to 6
- cache: bfloat16 [192, 2, 256, 1024], P(('sec', 'grp'), None, None, 'tp'), may hold values from -20 to 20
- lengths: int32 [192], P(('sec', 'grp')), may hold values from 16 to 256, as said below
- norm_gain: float32 [6144], replicated, may hold values from 0.25 to 1.75
- router: float32 [6144, 8], replicated, may hold values from -0.078125 to 0.078125
- route_ids: int32 [192, 2], P(('sec', 'grp')), may hold values from 0 to 7, all different within a row; in each aligned block of 6 rows (0 to 5, 6 to 11, ...) at most 3 rows name the same one
- w_gate: bfloat16 [8, 6144, 8192], P('grp', None, ('sec', 'tp')), may hold values from -0.078125 to 0.078125
- w_up: bfloat16 [8, 6144, 8192], P('grp', None, ('sec', 'tp')), may hold values from -0.078125 to 0.078125
- w_down: bfloat16 [8, 8192, 6144], P('grp', ('sec', 'tp')), may hold values from -0.0625 to 0.0625
Outputs:
- resid_out: bfloat16 [192, 6144], P(('sec', 'grp'), 'tp')
The draws below stay inside these ranges and needn't reach their ends.
Inputs may be any that keep to these rules, and one draw needn't show every extreme that they name: `route_ids`: each row names 2 different experts; in each aligned block of 6 rows, the rows of one micro-batch of one device, no expert is named by more than 3 rows. `lengths`: some sequence has all 256 slots valid.
All inputs are finite; a program needn't handle non-finite values.
Results may differ from the reference program's by a relative error of at most 0.006.
Values may be sent and summed in bfloat16 or wider, within the bound.
No kernel may reach another device: no remote copies, remote signals or barrier semaphores. Data moves between devices by JAX's collectives and lax.ppermute only.
A program may use at most 192 MiB of HBM per device.

```python
import math
import jax
import jax.numpy as jnp
import numpy as np
from jax import lax

D = 6144
HEADS = 48
KV_HEADS = 8
HEAD_DIM = 128
EXPERTS = 8
TOP = 2
FF = 8192
CACHE = 256
MB_ROWS = 6
CAP = 3
SPLIT = 1
TOKENS = 192


def draw_queries(key, part):
    key = jax.random.fold_in(key, 21)
    group_size = HEADS // KV_HEADS
    sampled = jnp.clip(jax.random.normal(key, (TOKENS, KV_HEADS, group_size, HEAD_DIM), jnp.float32), -6.0, 6.0)
    return sampled.reshape(TOKENS, HEADS * HEAD_DIM).astype(jnp.bfloat16)


def draw_cache(key, part):
    key = jax.random.fold_in(key, 22)
    sampled = jnp.clip(jax.random.normal(key, (TOKENS, 2, CACHE, KV_HEADS, HEAD_DIM), jnp.float32), -6.0, 6.0)
    return sampled.reshape(TOKENS, 2, CACHE, KV_HEADS * HEAD_DIM).astype(jnp.bfloat16)


def draw_lengths(key, part):
    key = jax.random.fold_in(key, 23)
    drawn = jax.random.randint(key, (TOKENS,), CACHE // 16, CACHE + 1)
    return jnp.where(jnp.arange(TOKENS) == 0, CACHE, drawn).astype(jnp.int32)


def block_levels(key, dims, split, low, high):
    def one(dim, blocks):
        steps = jax.random.uniform(jax.random.fold_in(jax.random.fold_in(key, 6), dim), (blocks,), jnp.float32, low / len(split), high / len(split))
        return jnp.repeat(jnp.exp(steps), dims[dim] // blocks).reshape((-1,) + (1,) * (len(dims) - dim - 1))

    loudness = one(*split[0])
    for cut in split[1:]:
        loudness = loudness * one(*cut)
    return loudness


def assign_block(key, own, number, rows, amount, top, bound, slope):
    ranking = jax.random.permutation(key, amount)
    packed, ordinary = portions_of(amount, rows * top, bound, slope, True), portions_of(amount, rows * top, bound, slope, False)
    places = jnp.arange(amount)

    def named(sizes, rotation):
        used = int((sizes > 0).sum())
        fixed = max(1, used // 4)
        moved = fixed + (places - fixed + rotation * (used - fixed)) % max(1, amount - fixed)
        return jnp.zeros((amount,), jnp.int32).at[ranking[jnp.where(places < fixed, places, moved)]].set(jnp.asarray(sizes, jnp.int32))

    sizes = jnp.where(number % 4 == 0, named(packed, number // 4), named(ordinary, number - number // 4 - 1))
    mixed = jax.random.permutation(jax.random.fold_in(own, 3), amount)
    source_of, sink = mixed[0:amount // 2 * 2:2], mixed[1:amount // 2 * 2:2]
    margin = jnp.minimum(sizes[source_of] - 1, bound - sizes[sink]) // 2
    margin = jnp.where((source_of == ranking[0]) | (sink == ranking[0]) | (sizes[sink] == 0), 0, jnp.maximum(margin, 0))
    moved = jax.random.randint(jax.random.fold_in(own, 4), (amount // 2,), 0, 1 << 20) % (margin + 1)
    sizes = sizes.at[source_of].add(-moved).at[sink].add(moved)
    members = jnp.searchsorted(jnp.cumsum(sizes), jnp.arange(rows * top), side="right").astype(jnp.int32)
    grid = members.reshape(top, rows).T
    grid = grid[jax.random.permutation(jax.random.fold_in(own, 1), rows)]
    rotation = jax.random.randint(jax.random.fold_in(own, 2), (rows, 1), 0, top)
    return jnp.take_along_axis(grid, (jnp.arange(top)[None, :] + rotation) % top, axis=1)


def portions_of(amount, total, most, skew, full):
    portions = [(1 << 20) // math.isqrt(grade ** skew) + 1 for grade in range(1, amount + 1)]
    largest = most if full else min(most, max(-(-total // amount), total * portions[0] // sum(portions)))
    least = 1 if total - largest >= amount - 1 else 0
    holding, rest = [largest] + [least] * (amount - 1), total - largest - least * (amount - 1)
    while rest > 0:
        movable = [i for i in range(1, amount) if holding[i] < largest] or [i for i in range(1, amount) if holding[i] < most]
        mass, remaining = sum([portions[i] for i in movable]), rest
        for i in movable:
            extra = min(most - holding[i], max(1, remaining * portions[i] // mass), rest)
            holding[i] = holding[i] + extra
            rest = rest - extra
    return np.array(holding)


def normal_values(key, shape, deviation, most, cuts=(), held_as=jnp.bfloat16):
    gain = block_levels(key, shape, cuts, -0.22, 0.18) if cuts else 1.0
    array = jax.random.normal(key, shape, jnp.float32) * deviation * gain
    return jnp.minimum(jnp.maximum(array, -most), most).astype(held_as)


def setup_inputs(seed: int = 0) -> dict:
    streams_of = jax.random.split(jax.random.key(seed), 12)
    resid_in = normal_values(streams_of[0], (TOKENS, D), 1.0, 6.0, ((0, 8), (1, 4)))
    queries = draw_queries(jax.random.fold_in(streams_of[11], 71), 0)
    new_kv = normal_values(streams_of[2], (TOKENS, 2, KV_HEADS * HEAD_DIM), 1.0, 6.0, ((0, 8), (2, 4)))
    cache = draw_cache(jax.random.fold_in(streams_of[11], 71), 0)
    lengths = draw_lengths(jax.random.fold_in(streams_of[11], 71), 0)
    norm_gain = jnp.clip(1.0 + 0.15 * jax.random.normal(streams_of[5], (D,), jnp.float32), 0.25, 1.75)
    router = normal_values(streams_of[6], (D, EXPERTS), D ** -0.5, 0.078125, (), jnp.float32)
    route_ids_keys = jax.random.split(jax.random.fold_in(streams_of[7], 1), TOKENS // MB_ROWS)
    route_ids_turns = jax.random.permutation(jax.random.fold_in(streams_of[7], 3), TOKENS // MB_ROWS)
    route_ids = jax.vmap(lambda own, number: assign_block(jax.random.fold_in(streams_of[7], 2), own, number, MB_ROWS, EXPERTS, TOP, CAP, 2))(route_ids_keys, route_ids_turns).reshape((TOKENS, TOP))
    w_gate = normal_values(streams_of[8], (EXPERTS * SPLIT, D, FF // SPLIT), D ** -0.5, 0.078125, ((0, 4), (2, 8)))
    w_up = normal_values(streams_of[9], (EXPERTS * SPLIT, D, FF // SPLIT), D ** -0.5, 0.078125, ((0, 4), (2, 8)))
    w_down = normal_values(streams_of[10], (EXPERTS * SPLIT, FF // SPLIT, D), FF ** -0.5, 0.0625, ((0, 4), (1, 8)))
    return dict(resid_in=resid_in, queries=queries, new_kv=new_kv, cache=cache, lengths=lengths, norm_gain=norm_gain, router=router, route_ids=route_ids, w_gate=w_gate, w_up=w_up, w_down=w_down)


epsilon = 1e-05

def attend(query_rows, cached_keys, cached_values, new_key, new_value, seq_lengths):
    factor = 1.0 / math.sqrt(query_rows.shape[-1])
    query_f = query_rows.astype(jnp.float32)
    scores = jnp.einsum('nkgd,nckd->nkgc', query_f, cached_keys.astype(jnp.float32)) * factor
    fresh_score = jnp.einsum('nkgd,nkd->nkg', query_f, new_key.astype(jnp.float32)) * factor
    valid_mask = (jnp.arange(cached_keys.shape[1])[None, :] < seq_lengths[:, None])[:, None, None, :]
    masked = jnp.where(valid_mask, scores, -jnp.inf)
    largest = jnp.maximum(lax.optimization_barrier(jnp.max(masked, axis=-1)), fresh_score)
    raw_weights = jnp.where(valid_mask, jnp.exp(masked - largest[..., None]), 0.0)
    fresh_weight = jnp.exp(fresh_score - largest)
    denominator = lax.optimization_barrier(jnp.sum(raw_weights, axis=-1)) + fresh_weight
    probabilities = (raw_weights / denominator[..., None]).astype(jnp.bfloat16)
    fresh_prob = (fresh_weight / denominator).astype(jnp.bfloat16)
    output = jnp.einsum('nkgc,nckd->nkgd', probabilities.astype(jnp.float32), cached_values.astype(jnp.float32))
    output = output + fresh_prob.astype(jnp.float32)[..., None] * new_value.astype(jnp.float32)[:, :, None, :]
    return output.astype(jnp.bfloat16).reshape(query_rows.shape[0], -1)

def reference(resid_in, queries, new_kv, cache, lengths, norm_gain, router, route_ids, w_gate, w_up, w_down):
    group_size = HEADS // KV_HEADS
    blocks = TOKENS // MB_ROWS

    def attend_block(pieces):
        query_b, fresh_batch_value, cache_b, length_b = pieces
        query_q = query_b.reshape(MB_ROWS, KV_HEADS, group_size, HEAD_DIM)
        fresh_q = fresh_batch_value.reshape(MB_ROWS, 2, KV_HEADS, HEAD_DIM)
        cache_q = cache_b.reshape(MB_ROWS, 2, CACHE, KV_HEADS, HEAD_DIM)
        return attend(query_q, cache_q[:, 0], cache_q[:, 1], fresh_q[:, 0], fresh_q[:, 1], length_b)
    attended = lax.map(attend_block, (queries.reshape(blocks, MB_ROWS, HEADS * HEAD_DIM), new_kv.reshape(blocks, MB_ROWS, 2, KV_HEADS * HEAD_DIM), cache.reshape(blocks, MB_ROWS, 2, CACHE, KV_HEADS * HEAD_DIM), lengths.reshape(blocks, MB_ROWS))).reshape(TOKENS, D)
    hidden = resid_in.astype(jnp.float32) + attended.astype(jnp.float32)
    row_scaling = lax.rsqrt(lax.optimization_barrier(jnp.mean(hidden * hidden, axis=1, keepdims=True)) + epsilon)
    normed = (hidden * row_scaling * norm_gain).astype(jnp.bfloat16)
    logits = jnp.dot(normed.astype(jnp.float32), router, precision=lax.Precision.HIGHEST)
    picked = jnp.take_along_axis(logits, route_ids, axis=1)
    first_mix = 1.0 / (1.0 + jnp.exp(picked[:, 1] - picked[:, 0]))
    second_mix = 1.0 / (1.0 + jnp.exp(picked[:, 0] - picked[:, 1]))
    limit = CAP * blocks
    gate_blocks = w_gate.reshape(EXPERTS, SPLIT, D, FF // SPLIT)
    up_blocks = w_up.reshape(EXPERTS, SPLIT, D, FF // SPLIT)
    down_blocks = w_down.reshape(EXPERTS, SPLIT, FF // SPLIT, D)

    def one_expert(running, pieces):
        gate_w, up_w, down_w, expert = pieces
        first_hit = route_ids[:, 0] == expert
        second_hit = route_ids[:, 1] == expert
        weight_row = jnp.where(first_hit, first_mix, 0.0) + jnp.where(second_hit, second_mix, 0.0)
        member = (first_hit | second_hit).astype(jnp.int32)
        row_order = jnp.argsort(1 - member, stable=True)[:limit].astype(jnp.int32)
        chosen_rows = normed[row_order].astype(jnp.float32)
        gate_value = jnp.einsum('td,sdf->tsf', chosen_rows, gate_w.astype(jnp.float32))
        up_value = jnp.einsum('td,sdf->tsf', chosen_rows, up_w.astype(jnp.float32))
        activated = (jax.nn.silu(gate_value) * up_value).astype(jnp.bfloat16)
        result = jnp.einsum('tsf,sfd->td', activated.astype(jnp.float32), down_w.astype(jnp.float32))
        return (running.at[row_order].add(result * weight_row[row_order][:, None]), None)
    running, unused = lax.scan(one_expert, jnp.zeros((TOKENS, D), jnp.float32), (gate_blocks, up_blocks, down_blocks, jnp.arange(EXPERTS, dtype=jnp.int32)))
    return (hidden + running).astype(jnp.bfloat16)
```

```python
import functools
import math

import jax
import jax.numpy as jnp
from jax import lax
from jax.experimental import pallas as pl
from jax.experimental.pallas import tpu as pltpu
from jax.sharding import PartitionSpec as P

HEAD_DIM = 128
ROWS_STEP = 8
MIB = 1 << 20

epsilon = 1e-05


def largest_divisor(total, choices):
    return next(c for c in choices if total % c == 0)


def attend_kernel(lengths_ref, query_ref, new_ref, resid_ref, cache_ref, attended_ref, hidden_ref, *, kv_local, group):
    step = pl.program_id(0)
    rows = ROWS_STEP
    cache_len = cache_ref.shape[2]
    stacked = group * rows
    factor = 1.0 / math.sqrt(HEAD_DIM)
    row_of = lax.broadcasted_iota(jnp.int32, (stacked, 1), 0) % rows
    length_col = jnp.zeros((stacked, 1), jnp.int32)
    for n in range(rows):
        length_col = jnp.where(row_of == n, lengths_ref[step * rows + n], length_col)
    valid = lax.broadcasted_iota(jnp.int32, (stacked, cache_len), 1) < length_col
    for head in range(kv_local):
        lanes = pl.ds(head * HEAD_DIM, HEAD_DIM)
        first = head * group
        query = jnp.concatenate(
            [
                query_ref[:, pl.ds((first + g) * HEAD_DIM, HEAD_DIM)].astype(jnp.float32)
                for g in range(group)
            ],
            axis=0,
        )
        query_bf = query.astype(jnp.bfloat16)
        new_key = new_ref[:, 0, lanes].astype(jnp.float32)
        new_value = new_ref[:, 1, lanes].astype(jnp.float32)
        scores = jnp.zeros((stacked, cache_len), jnp.float32)
        for n in range(rows):
            full = lax.dot_general(
                query_bf,
                cache_ref[n, 0, :, lanes],
                (((1,), (1,)), ((), ())),
                preferred_element_type=jnp.float32,
            )
            scores = jnp.where(row_of == n, full, scores)
        scores = jnp.where(valid, scores * factor, -jnp.inf)
        fresh = (
            jnp.sum(query * jnp.concatenate([new_key] * group, axis=0), axis=1, keepdims=True)
            * factor
        )
        largest = jnp.maximum(jnp.max(scores, axis=1, keepdims=True), fresh)
        weights = jnp.exp(scores - largest)
        fresh_weight = jnp.exp(fresh - largest)
        denominator = jnp.sum(weights, axis=1, keepdims=True) + fresh_weight
        probabilities = (weights / denominator).astype(jnp.bfloat16)
        fresh_prob = (fresh_weight / denominator).astype(jnp.bfloat16).astype(jnp.float32)
        output = jnp.zeros((stacked, HEAD_DIM), jnp.float32)
        for n in range(rows):
            full = jnp.dot(
                probabilities, cache_ref[n, 1, :, lanes], preferred_element_type=jnp.float32
            )
            output = jnp.where(row_of == n, full, output)
        output = output + fresh_prob * jnp.concatenate([new_value] * group, axis=0)
        attended = output.astype(jnp.bfloat16)
        for g in range(group):
            columns = pl.ds((first + g) * HEAD_DIM, HEAD_DIM)
            piece = output[g * rows : (g + 1) * rows].astype(jnp.bfloat16)
            attended_ref[:, columns] = piece
            hidden_ref[:, columns] = (
                resid_ref[:, columns].astype(jnp.float32) + piece.astype(jnp.float32)
            ).astype(jnp.bfloat16)


def attend(lengths, queries, new_kv, resid_in, cache):
    sequences, part_cols = queries.shape
    cache_len, kv_cols = cache.shape[2:]
    kv_local = kv_cols // HEAD_DIM
    group = part_cols // kv_cols
    rows = ROWS_STEP
    flat = pl.BlockSpec((rows, part_cols), lambda i, _: (i, 0))
    return pl.pallas_call(
        functools.partial(attend_kernel, kv_local=kv_local, group=group),
        grid_spec=pltpu.PrefetchScalarGridSpec(
            num_scalar_prefetch=1,
            grid=(sequences // rows,),
            in_specs=[
                flat,
                pl.BlockSpec((rows, 2, kv_cols), lambda i, _: (i, 0, 0)),
                flat,
                pl.BlockSpec((rows, 2, cache_len, kv_cols), lambda i, _: (i, 0, 0, 0)),
            ],
            out_specs=[flat, flat],
        ),
        out_shape=[jax.ShapeDtypeStruct((sequences, part_cols), jnp.bfloat16)] * 2,
        compiler_params=pltpu.CompilerParams(vmem_limit_bytes=16 * MIB),
        name="attend",
    )(lengths, queries, new_kv, resid_in, cache)


def experts_kernel(
    place_ref, gain_ref, router_ref, gate_hbm, up_hbm, down_hbm, *rest, pieces, rows, part_cols, tps, split, kb, nb, depth_in, depth_out
):
    piece_refs = rest[:pieces]
    out_refs = rest[pieces : 2 * pieces]
    gate_buf, up_buf, down_buf, acc_gate, acc_up, act_ref, in_sem, out_sem = rest[2 * pieces :]
    held, width, ff = gate_hbm.shape
    tokens = pieces * rows
    experts = router_ref.shape[0]
    grp, tp = place_ref[0], place_ref[1]
    per_part = part_cols // kb
    in_steps = width // kb
    out_per_part = part_cols // nb
    out_steps = width // nb

    def offset_in(k):
        return pl.multiple_of((k // per_part ^ tp) * part_cols + k % per_part * kb, kb)

    def offset_out(k):
        return pl.multiple_of((k // out_per_part ^ tp) * part_cols + k % out_per_part * nb, nb)

    def in_copies(k):
        slot = lax.rem(k, depth_in)
        source = pl.ds(offset_in(k), kb)
        found = []
        for e in range(held):
            found.append(
                pltpu.make_async_copy(gate_hbm.at[e, source], gate_buf.at[slot, e], in_sem.at[slot, 2 * e])
            )
            found.append(
                pltpu.make_async_copy(up_hbm.at[e, source], up_buf.at[slot, e], in_sem.at[slot, 2 * e + 1])
            )
        return found

    def out_copies(k):
        slot = lax.rem(k, depth_out)
        source = pl.ds(offset_out(k), nb)
        return [
            pltpu.make_async_copy(down_hbm.at[e, :, source], down_buf.at[slot, pl.ds(e * ff, ff)], out_sem.at[slot, e])
            for e in range(held)
        ]

    for k in range(min(depth_in, in_steps)):
        for copy in in_copies(k):
            copy.start()
    for k in range(min(depth_out, out_steps)):
        for copy in out_copies(k):
            copy.start()
    acc_gate[...] = jnp.zeros_like(acc_gate)
    acc_up[...] = jnp.zeros_like(acc_up)

    def in_body(k, carry):
        squares, logits = carry
        local = pl.ds(pl.multiple_of(k * kb, kb), kb)
        there = pl.ds(offset_in(k), kb)
        slot = lax.rem(k, depth_in)
        raw = jnp.concatenate([ref[:, local].astype(jnp.float32) for ref in piece_refs], axis=0)
        squares = squares + jnp.sum(raw * raw, axis=1, keepdims=True)
        scaled = (raw * gain_ref[:, there]).astype(jnp.bfloat16)
        router = router_ref[:, there]
        high = router.astype(jnp.bfloat16)
        low = (router - high.astype(jnp.float32)).astype(jnp.bfloat16)
        for part in (high, low):
            logits = logits + lax.dot_general(
                scaled, part, (((1,), (1,)), ((), ())), preferred_element_type=jnp.float32
            )
        for copy in in_copies(k):
            copy.wait()
        for e in range(held):
            acc_gate[e] += jnp.dot(scaled, gate_buf[slot, e], preferred_element_type=jnp.float32)
            acc_up[e] += jnp.dot(scaled, up_buf[slot, e], preferred_element_type=jnp.float32)

        @pl.when(k + depth_in < in_steps)
        def _():
            for copy in in_copies(k + depth_in):
                copy.start()

        return squares, logits

    squares, logits = lax.fori_loop(
        0,
        in_steps,
        in_body,
        (jnp.zeros((tokens, 1), jnp.float32), jnp.zeros((tokens, experts), jnp.float32)),
    )
    row_scale = lax.rsqrt(squares / width + epsilon)
    logits = logits * row_scale
    ids = jnp.concatenate([ref[:, pl.ds(width, 128)].astype(jnp.float32) for ref in piece_refs], axis=0)
    names = [ids[:, k : k + 1].astype(jnp.int32) for k in range(2)]
    lane = lax.broadcasted_iota(jnp.int32, (tokens, experts), 1)
    picked = [jnp.sum(jnp.where(lane == name, logits, 0.0), axis=1, keepdims=True) for name in names]
    mixes = [
        1.0 / (1.0 + jnp.exp(picked[1] - picked[0])),
        1.0 / (1.0 + jnp.exp(picked[0] - picked[1])),
    ]
    for e in range(held):
        expert = (grp * held + e) // split
        share = sum(jnp.where(name == expert, mix, 0.0) for name, mix in zip(names, mixes))
        gate = acc_gate[e] * row_scale
        up = acc_up[e] * (row_scale * share)
        act_ref[:, pl.ds(e * ff, ff)] = (gate / (1.0 + jnp.exp(-gate)) * up).astype(jnp.bfloat16)

    def out_body(k, carry):
        slot = lax.rem(k, depth_out)
        for copy in out_copies(k):
            copy.wait()
        partial = jnp.dot(act_ref[...], down_buf[slot], preferred_element_type=jnp.float32)
        columns = pl.ds(pl.multiple_of(k * nb, nb), nb)
        for p, ref in enumerate(out_refs):
            ref[:, columns] = partial[p * rows : (p + 1) * rows].astype(jnp.bfloat16)

        @pl.when(k + depth_out < out_steps)
        def _():
            for copy in out_copies(k + depth_out):
                copy.start()

        return carry

    lax.fori_loop(0, out_steps, out_body, 0)


def run_experts(place, norm_gain, router, w_gate, w_up, w_down, pieces, part_cols, tps, split):
    held, width, ff = w_gate.shape
    rows = pieces[0].shape[0]
    count = len(pieces)
    tokens = rows * count
    kb = largest_divisor(part_cols, (512, 384, 256, 128))
    nb = largest_divisor(part_cols, (512, 384, 256, 128))
    depth_in, depth_out = 3, 4
    vmem = pl.BlockSpec(memory_space=pltpu.VMEM)
    hbm = pl.BlockSpec(memory_space=pltpu.HBM)
    return pl.pallas_call(
        functools.partial(
            experts_kernel,
            pieces=count,
            rows=rows,
            part_cols=part_cols,
            tps=tps,
            split=split,
            kb=kb,
            nb=nb,
            depth_in=depth_in,
            depth_out=depth_out,
        ),
        in_specs=[pl.BlockSpec(memory_space=pltpu.SMEM), vmem, vmem, hbm, hbm, hbm] + [vmem] * count,
        out_specs=[vmem] * count,
        out_shape=[jax.ShapeDtypeStruct((rows, width), jnp.bfloat16)] * count,
        scratch_shapes=[
            pltpu.VMEM((depth_in, held, kb, ff), jnp.bfloat16),
            pltpu.VMEM((depth_in, held, kb, ff), jnp.bfloat16),
            pltpu.VMEM((depth_out, held * ff, nb), jnp.bfloat16),
            pltpu.VMEM((held, tokens, ff), jnp.float32),
            pltpu.VMEM((held, tokens, ff), jnp.float32),
            pltpu.VMEM((tokens, held * ff), jnp.bfloat16),
            pltpu.SemaphoreType.DMA((depth_in, 2 * held)),
            pltpu.SemaphoreType.DMA((depth_out, held)),
        ],
        compiler_params=pltpu.CompilerParams(vmem_limit_bytes=52 * MIB),
        name="experts",
    )(place, norm_gain.reshape(1, width), router.T, w_gate, w_up, w_down, *pieces)


def swap(array, axis, offset):
    size = lax.axis_size(axis)
    return lax.ppermute(array, axis, [(i, i ^ offset) for i in range(size)])


def on_device(
    resid_in, queries, new_kv, cache, lengths, norm_gain, router, route_ids, w_gate, w_up, w_down
):
    sequences, part_cols = resid_in.shape
    tps, grps, secs = lax.axis_size("tp"), lax.axis_size("grp"), lax.axis_size("sec")
    held = w_gate.shape[0]
    split = max(1, grps * held // router.shape[1])
    place = jnp.stack([lax.axis_index("grp"), lax.axis_index("tp")]).astype(jnp.int32)

    attended, hidden = attend(lengths, queries, new_kv, resid_in, cache)

    ids = jnp.pad(route_ids.astype(jnp.bfloat16), ((0, 0), (0, 128 - route_ids.shape[1])))
    columns = [hidden] + [swap(hidden, "tp", j) for j in range(1, tps)]
    own = jnp.concatenate(columns + [ids], axis=1)
    near = [own] + [swap(own, "grp", d) for d in range(1, grps)]
    pieces = near + [swap(piece, "sec", s) for s in range(1, secs) for piece in near]

    partial = run_experts(
        place, norm_gain, router, w_gate, w_up, w_down, pieces, part_cols, tps, split
    )

    def total(arrays):
        result = arrays[0].astype(jnp.float32)
        for array in arrays[1:]:
            result = result + array.astype(jnp.float32)
        return result

    sums = []
    for d in range(grps):
        terms = [partial[d]] + [swap(partial[s * grps + d], "sec", s) for s in range(1, secs)]
        sums.append(total(terms).astype(jnp.bfloat16))
    rows_sum = total([sums[0]] + [swap(sums[d], "grp", d) for d in range(1, grps)])
    parts = [
        rows_sum[:, j * part_cols : (j + 1) * part_cols].astype(jnp.bfloat16) for j in range(tps)
    ]
    mixed = total([parts[0]] + [swap(parts[j], "tp", j) for j in range(1, tps)])
    hidden_part = resid_in.astype(jnp.float32) + attended.astype(jnp.float32)
    return (hidden_part + mixed).astype(jnp.bfloat16)


def solution(mesh):
    return jax.shard_map(
        on_device,
        mesh=mesh,
        in_specs=(
            P(("sec", "grp"), "tp"),
            P(("sec", "grp"), "tp"),
            P(("sec", "grp"), None, "tp"),
            P(("sec", "grp"), None, None, "tp"),
            P(("sec", "grp")),
            P(),
            P(),
            P(("sec", "grp"), None),
            P("grp", None, ("sec", "tp")),
            P("grp", None, ("sec", "tp")),
            P("grp", ("sec", "tp"), None),
        ),
        out_specs=P(("sec", "grp"), "tp"),
        check_vma=False,
    )
```

```python
import functools
import math

import jax
import jax.numpy as jnp
from jax import lax
from jax.experimental import pallas as pl
from jax.experimental.pallas import tpu as pltpu
from jax.sharding import PartitionSpec as P

HEAD_DIM = 128
ROWS_STEP = 8
MIB = 1 << 20
VMEM_GATE_UP = 22

epsilon = 1e-05


def largest_divisor(total, choices):
    return next(c for c in choices if total % c == 0)


def attend_kernel(lengths_ref, query_ref, new_ref, resid_ref, cache_ref, attended_ref, hidden_ref, *, heads, group):
    step = pl.program_id(0)
    rows = ROWS_STEP
    cache_len = cache_ref.shape[2]
    factor = 1.0 / math.sqrt(HEAD_DIM)
    for kv_head, lead, count in heads:
        stacked = count * rows
        row_of = lax.broadcasted_iota(jnp.int32, (stacked, 1), 0) % rows
        length_col = jnp.zeros((stacked, 1), jnp.int32)
        for n in range(rows):
            length_col = jnp.where(row_of == n, lengths_ref[step * rows + n], length_col)
        valid = lax.broadcasted_iota(jnp.int32, (stacked, cache_len), 1) < length_col
        lanes = pl.ds(kv_head * HEAD_DIM, HEAD_DIM)
        columns = [pl.ds((lead + g) * HEAD_DIM, HEAD_DIM) for g in range(count)]
        query = jnp.concatenate([query_ref[:, c].astype(jnp.float32) for c in columns], axis=0)
        query_bf = query.astype(jnp.bfloat16)
        new_key = new_ref[:, 0, lanes].astype(jnp.float32)
        new_value = new_ref[:, 1, lanes].astype(jnp.float32)
        scores = jnp.zeros((stacked, cache_len), jnp.float32)
        for n in range(rows):
            full = lax.dot_general(
                query_bf,
                cache_ref[n, 0, :, lanes],
                (((1,), (1,)), ((), ())),
                preferred_element_type=jnp.float32,
            )
            scores = jnp.where(row_of == n, full, scores)
        scores = jnp.where(valid, scores * factor, -jnp.inf)
        fresh = (
            jnp.sum(query * jnp.concatenate([new_key] * count, axis=0), axis=1, keepdims=True) * factor
        )
        largest = jnp.maximum(jnp.max(scores, axis=1, keepdims=True), fresh)
        weights = jnp.exp(scores - largest)
        fresh_weight = jnp.exp(fresh - largest)
        denominator = jnp.sum(weights, axis=1, keepdims=True) + fresh_weight
        probabilities = (weights / denominator).astype(jnp.bfloat16)
        fresh_prob = (fresh_weight / denominator).astype(jnp.bfloat16).astype(jnp.float32)
        output = jnp.zeros((stacked, HEAD_DIM), jnp.float32)
        for n in range(rows):
            full = jnp.dot(
                probabilities, cache_ref[n, 1, :, lanes], preferred_element_type=jnp.float32
            )
            output = jnp.where(row_of == n, full, output)
        output = output + fresh_prob * jnp.concatenate([new_value] * count, axis=0)
        for g, c in enumerate(columns):
            piece = output[g * rows : (g + 1) * rows].astype(jnp.bfloat16)
            attended_ref[:, c] = piece
            hidden_ref[:, c] = (
                resid_ref[:, c].astype(jnp.float32) + piece.astype(jnp.float32)
            ).astype(jnp.bfloat16)


def attend(lengths, queries, new_kv, resid_in, cache, chunk, chunks):
    sequences, part_cols = queries.shape
    cache_len, kv_cols = cache.shape[2:]
    kv_local = kv_cols // HEAD_DIM
    group = part_cols // kv_cols
    rows = ROWS_STEP
    width = part_cols // chunks
    count = width // HEAD_DIM
    lead = chunk * count
    spans = [
        (kv, max(kv * group, lead), min((kv + 1) * group, lead + count)) for kv in range(kv_local)
    ]
    spans = [span for span in spans if span[1] < span[2]]
    first_kv = spans[0][0]
    lanes = (spans[-1][0] - first_kv + 1) * HEAD_DIM
    assert kv_cols % lanes == 0 and first_kv * HEAD_DIM % lanes == 0
    heads = [(kv - first_kv, start - lead, stop - start) for kv, start, stop in spans]
    block = first_kv * HEAD_DIM // lanes

    def flat(index):
        return pl.BlockSpec((rows, width), lambda i, _: (i, index))

    return pl.pallas_call(
        functools.partial(attend_kernel, heads=heads, group=group),
        grid_spec=pltpu.PrefetchScalarGridSpec(
            num_scalar_prefetch=1,
            grid=(sequences // rows,),
            in_specs=[
                flat(chunk),
                pl.BlockSpec((rows, 2, lanes), lambda i, _: (i, 0, block)),
                flat(chunk),
                pl.BlockSpec((rows, 2, cache_len, lanes), lambda i, _: (i, 0, 0, block)),
            ],
            out_specs=[flat(0)] * 2,
        ),
        out_shape=[jax.ShapeDtypeStruct((sequences, width), jnp.bfloat16)] * 2,
        cost_estimate=pl.CostEstimate(
            flops=0, bytes_accessed=2 * cache.size // chunks, transcendentals=0
        ),
        compiler_params=pltpu.CompilerParams(vmem_limit_bytes=32 * MIB),
        name="attend",
    )(lengths, *(pin(array, pltpu.HBM) for array in (queries, new_kv, resid_in, cache)))


def fetch_kernel(after_ref, earlier_ref, source_hbm, *rest, index, extras):
    extra_hbm, (target_ref, token_ref, *extra_refs, sem) = rest[:extras], rest[extras:]
    pieces = sem.shape[0] - extras
    step = target_ref.shape[0] // pieces
    copies = [
        pltpu.make_async_copy(source, target, sem.at[pieces + i])
        for i, (source, target) in enumerate(zip(extra_hbm, extra_refs))
    ]
    copies += [
        pltpu.make_async_copy(
            source_hbm.at[index, pl.ds(i * step, step)], target_ref.at[pl.ds(i * step, step)], sem.at[i]
        )
        for i in range(pieces)
    ]
    for copy in copies:
        copy.start()
    token_ref[...] = jnp.zeros_like(token_ref)
    for copy in copies:
        copy.wait()


def fetch(after, earlier, weights, index, extra=()):
    shape = weights.shape[1:]
    pieces = 8
    hbm = pl.BlockSpec(memory_space=pltpu.HBM)
    return pl.pallas_call(
        functools.partial(fetch_kernel, index=index, extras=len(extra)),
        in_specs=[pl.BlockSpec(memory_space=pl.ANY)] * 2 + [hbm] * (1 + len(extra)),
        out_specs=[pl.BlockSpec(memory_space=pltpu.VMEM)] * (2 + len(extra)),
        out_shape=[pltpu.VMEM(shape, weights.dtype), pltpu.VMEM((8, 128), jnp.float32)]
        + [pltpu.VMEM(array.shape, array.dtype) for array in extra],
        scratch_shapes=[pltpu.SemaphoreType.DMA((pieces + len(extra),))],
        cost_estimate=pl.CostEstimate(flops=0, bytes_accessed=2 * math.prod(shape), transcendentals=0),
        compiler_params=pltpu.CompilerParams(vmem_limit_bytes=1 * MIB),
        name="fetch",
    )(after, earlier, *(pin(array, pltpu.HBM) for array in (weights, *extra)))


def norm_kernel(gain_ref, router_ref, ids_ref, *rest):
    part_refs, own_ref = rest[:-1], rest[-1]
    tps = len(part_refs)
    rows, part_cols = part_refs[0].shape
    width = tps * part_cols
    experts = router_ref.shape[0]
    tp = lax.axis_index("tp")
    places = [pl.ds(pl.multiple_of((j ^ tp) * part_cols, 128), part_cols) for j in range(tps)]
    raws = [ref[...].astype(jnp.float32) for ref in part_refs]
    squares = sum(jnp.sum(raw * raw, axis=1, keepdims=True) for raw in raws)
    row_scale = lax.rsqrt(squares / width + epsilon)
    logits = jnp.zeros((rows, 2 * experts), jnp.float32)
    for raw, there in zip(raws, places):
        normed = (raw * row_scale * gain_ref[:, there]).astype(jnp.bfloat16)
        own_ref[:, there] = normed
        router = router_ref[:, there]
        high = router.astype(jnp.bfloat16).astype(jnp.float32)
        both = jnp.concatenate([high, router - high], axis=0).astype(jnp.bfloat16)
        logits += lax.dot_general(
            normed, both, (((1,), (1,)), ((), ())), preferred_element_type=jnp.float32
        )
    logits = logits[:, :experts] + logits[:, experts:]
    square = [lax.broadcasted_iota(jnp.int32, (rows, rows), axis) for axis in range(2)]
    identity = jnp.where(square[0] == square[1], 1.0, 0.0)
    ids = lax.dot_general(
        identity, ids_ref[...].astype(jnp.float32), (((1,), (1,)), ((), ())), preferred_element_type=jnp.float32
    ).astype(jnp.int32)
    names = [ids[:, k : k + 1] for k in range(2)]
    lane = lax.broadcasted_iota(jnp.int32, (rows, experts), 1)
    picked = [jnp.sum(jnp.where(lane == name, logits, 0.0), axis=1, keepdims=True) for name in names]
    mixes = [
        1.0 / (1.0 + jnp.exp(picked[1] - picked[0])),
        1.0 / (1.0 + jnp.exp(picked[0] - picked[1])),
    ]
    lane = lax.broadcasted_iota(jnp.int32, (rows, 128), 1)
    share = sum(jnp.where(lane % experts == name, mix, 0.0) for name, mix in zip(names, mixes))
    high = share.astype(jnp.bfloat16).astype(jnp.float32)
    own_ref[:, pl.ds(width, 128)] = jnp.where(lane < experts, high, share - high).astype(jnp.bfloat16)


def norm(gain, router, route_ids, parts):
    rows, part_cols = parts[0].shape
    vmem = pl.BlockSpec(memory_space=pltpu.VMEM)
    near = [pin(a, pltpu.VMEM) for a in (gain, router, route_ids, *parts)]
    return pl.pallas_call(
        norm_kernel,
        in_specs=[vmem] * len(near),
        out_specs=vmem,
        out_shape=pltpu.VMEM((rows, part_cols * len(parts) + 128), jnp.bfloat16),
        compiler_params=pltpu.CompilerParams(vmem_limit_bytes=2 * MIB),
        name="norm",
    )(*near)


def split_kernel(first_ref, second_ref, left_ref, right_ref):
    cut = left_ref.shape[1]
    left_ref[...] = first_ref[:, pl.ds(0, cut)]
    right_ref[...] = second_ref[:, pl.ds(cut, right_ref.shape[1])]


def split(first, second, cut):
    rows, width = first.shape
    vmem = pl.BlockSpec(memory_space=pltpu.VMEM)
    return pl.pallas_call(
        split_kernel,
        in_specs=[vmem] * 2,
        out_specs=[vmem] * 2,
        out_shape=[pltpu.VMEM((rows, cut), first.dtype), pltpu.VMEM((rows, width - cut), first.dtype)],
        compiler_params=pltpu.CompilerParams(vmem_limit_bytes=1 * MIB),
        name="split",
    )(pin(first, pltpu.VMEM), pin(second, pltpu.VMEM))


def gate_up_kernel(gate_hbm, up_hbm, token_ref, gate_ref, *rest, layout, experts, blocks_held, depth, nb):
    pieces = sum(layout)
    piece_refs, (act_ref, buf, rows_ref, sem) = rest[:pieces], rest[pieces:]
    held, width, ff = gate_hbm.shape
    ready = 1
    blocks = ff // nb
    deep = buf.shape[1]
    cuts = width // deep
    steps = (2 * held - ready) * blocks * cuts
    grp = lax.axis_index("grp")

    def block_copy(hbm, e, n, i):
        slot = lax.rem(i, depth)
        columns = pl.ds(pl.multiple_of(n * nb, 128), nb)
        there = pl.ds(pl.multiple_of(i % cuts * deep, 128), deep)
        return pltpu.make_async_copy(hbm.at[e, there, columns], buf.at[slot], sem.at[slot])

    def start(i):
        first = 0
        for e in range(held):
            kinds = (up_hbm,) if e < ready else (gate_hbm, up_hbm)
            for which, hbm in enumerate(kinds):
                inside = i // cuts - first
                hit = (inside >= 0) & (inside < len(kinds) * blocks) & (inside % len(kinds) == which)

                @pl.when(hit)
                def _():
                    block_copy(hbm, e, inside // len(kinds), i).start()

            first += len(kinds) * blocks

    def prime(i, carry):
        start(i)
        return carry

    lax.fori_loop(0, min(depth, steps), prime, 0)

    rows_of, first = [], 0
    for parts in layout:
        rows_of.append(piece_refs[first : first + parts])
        first += parts

    def gather(start_column, size):
        found = []
        for refs in rows_of:
            at = start_column
            for ref in refs:
                if at < ref.shape[1]:
                    found.append(ref[:, pl.ds(at, size)].astype(jnp.float32))
                    break
                at -= ref.shape[1]
        return jnp.concatenate(found, axis=0)

    for k in range(width // deep):
        rows_ref[:, pl.ds(k * deep, deep)] = gather(k * deep, deep).astype(jnp.bfloat16)
    shares = gather(width, 128)
    shares = shares[:, :experts] + shares[:, experts : 2 * experts]
    lane = lax.broadcasted_iota(jnp.int32, shares.shape, 1)

    def streamed(block):
        product = 0.0
        for cut in range(cuts):
            i = block * cuts + cut
            block_copy(gate_hbm, 0, 0, i).wait()
            there = pl.ds(cut * deep, deep)
            product += jnp.dot(
                rows_ref[:, there], buf[lax.rem(i, depth)], preferred_element_type=jnp.float32
            )

            @pl.when(i + depth < steps)
            def _():
                start(i + depth)

        return product

    first = 0
    for e in range(held):
        expert = (grp * held + e) // blocks_held
        share = jnp.sum(jnp.where(lane == expert, shares, 0.0), axis=1, keepdims=True)

        def body(n, carry, e=e, first=first, share=share):
            columns = pl.ds(pl.multiple_of(n * nb, 128), nb)
            if e < ready:
                i = first + n
                gate = jnp.dot(rows_ref[...], gate_ref[:, columns], preferred_element_type=jnp.float32)
            else:
                i = first + 2 * n + 1
                gate = streamed(i - 1)
            up = streamed(i) * share
            out = pl.ds(pl.multiple_of(e * ff + n * nb, 128), nb)
            act_ref[:, out] = (gate / (1.0 + jnp.exp(-gate)) * up).astype(jnp.bfloat16)
            return carry

        lax.fori_loop(0, blocks, body, 0)
        first += (1 if e < ready else 2) * blocks


def gate_up(w_gate, w_up, token, gate_ready, pieces, experts, blocks_held):
    held, width, ff = w_gate.shape
    tokens = sum(parts[0].shape[0] for parts in pieces)
    nb = largest_divisor(ff, (1024, 512, 256, 128))
    depth, cuts = 4, 4
    vmem = pl.BlockSpec(memory_space=pltpu.VMEM)
    hbm = pl.BlockSpec(memory_space=pltpu.HBM)
    near = [pin(a, pltpu.VMEM) for a in (gate_ready, *(part for parts in pieces for part in parts))]
    return pl.pallas_call(
        functools.partial(
            gate_up_kernel,
            layout=tuple(len(parts) for parts in pieces),
            experts=experts,
            blocks_held=blocks_held,
            depth=depth,
            nb=nb,
        ),
        in_specs=[hbm] * 2 + [pl.BlockSpec(memory_space=pl.ANY)] + [vmem] * len(near),
        out_specs=vmem,
        out_shape=pltpu.VMEM((tokens, held * ff), jnp.bfloat16),
        scratch_shapes=[
            pltpu.VMEM((depth, width // cuts, nb), jnp.bfloat16),
            pltpu.VMEM((tokens, width), jnp.bfloat16),
            pltpu.SemaphoreType.DMA((depth,)),
        ],
        cost_estimate=pl.CostEstimate(
            flops=4 * held * tokens * width * ff, bytes_accessed=4 * held * width * ff, transcendentals=0
        ),
        compiler_params=pltpu.CompilerParams(vmem_limit_bytes=VMEM_GATE_UP * MIB),
        name="gate_up",
    )(pin(w_gate, pltpu.HBM), pin(w_up, pltpu.HBM), token, *near)


def down_kernel(act_ref, *rest, first, part_cols, cuts):
    down_refs, (own_ref, other_ref) = rest[:-2], rest[-2:]
    ff = down_refs[0].shape[0]
    half = own_ref.shape[0]
    nb = part_cols // cuts
    tp = lax.axis_index("tp")

    def body(i, carry):
        j = first + i // cuts
        there = pl.ds(pl.multiple_of((j ^ tp) * part_cols + i % cuts * nb, 128), nb)
        partial = sum(
            jnp.dot(act_ref[:, pl.ds(e * ff, ff)], ref[:, there], preferred_element_type=jnp.float32)
            for e, ref in enumerate(down_refs)
        )
        columns = pl.ds(pl.multiple_of(i * nb, 128), nb)
        own_ref[:, columns] = partial[:half].astype(jnp.bfloat16)
        other_ref[:, columns] = partial[half:].astype(jnp.bfloat16)
        return carry

    lax.fori_loop(0, own_ref.shape[1] // nb, body, 0)


def down(act, weights, first, parts, part_cols, secs):
    tokens, depth = act.shape
    vmem = pl.BlockSpec(memory_space=pltpu.VMEM)
    near = [pin(a, pltpu.VMEM) for a in (act, *weights)]
    return pl.pallas_call(
        functools.partial(down_kernel, first=first, part_cols=part_cols, cuts=2),
        in_specs=[vmem] * len(near),
        out_specs=[vmem] * secs,
        out_shape=[pltpu.VMEM((tokens // secs, parts * part_cols), jnp.bfloat16)] * secs,
        cost_estimate=pl.CostEstimate(
            flops=2 * tokens * depth * parts * part_cols, bytes_accessed=0, transcendentals=0
        ),
        compiler_params=pltpu.CompilerParams(vmem_limit_bytes=4 * MIB),
        name="down",
    )(*near)


def pin(array, space):
    return pltpu.with_memory_space_constraint(array, space)


def swap(array, axis, offset):
    size = lax.axis_size(axis)
    return lax.ppermute(array, axis, [(i, i ^ offset) for i in range(size)])


def on_device(
    resid_in, queries, new_kv, cache, lengths, norm_gain, router, route_ids, w_gate, w_up, w_down
):
    sequences, part_cols = resid_in.shape
    tps, grps, secs = lax.axis_size("tp"), lax.axis_size("grp"), lax.axis_size("sec")
    held = w_gate.shape[0]
    blocks_held = max(1, grps * held // router.shape[1])
    tie = lax.optimization_barrier
    attended, hidden = attend(lengths, queries, new_kv, resid_in, cache, 0, 1)

    parts = [hidden] + [swap(hidden, "tp", j) for j in range(1, tps)]
    gain, router_rows = norm_gain.reshape(1, -1), router.T
    gate_ready, token, gain, router_rows, ids = fetch(
        hidden, hidden, w_gate, 0, (gain, router_rows, route_ids.T)
    )
    own = norm(gain, router_rows, ids, parts)
    down_ready = []
    if grps == 4:
        near = [own, swap(own, "grp", 1), swap(own, "grp", 2)]
        ready, token = fetch(own, token, w_down, 0)
        down_ready.append(ready)
        near, token = tie((near, token))
        after, right = split(near[2], near[1], tps // 2 * part_cols)
        across = [swap(after, "grp", 1), swap(right, "grp", 2)]
        near = [[array] for array in near]
    else:
        near = [[own]] + [[swap(own, "grp", d)] for d in range(1, grps - 1)]
        after = own
        across = [swap(own, "grp", grps - 1)]
    for e in range(len(down_ready), held):
        ready, token = fetch(after, token, w_down, e)
        down_ready.append(ready)
    across, token = tie((across, token))
    near.append(across)
    pieces = near + [[swap(array, "sec", 1) for array in arrays] for arrays in near]
    act = gate_up(w_gate, w_up, token, gate_ready, pieces, router.shape[1], blocks_held)

    def total(arrays):
        result = arrays[0].astype(jnp.float32)
        for array in arrays[1:]:
            result = result + array.astype(jnp.float32)
        return result

    halves = []
    for c in range(2):
        kept, sent = down(act, down_ready, c * tps // 2, tps // 2, part_cols, secs)
        act, _ = tie((act, sent))
        halves.append((kept, swap(sent, "sec", 1)))
    size = sequences
    sums = [
        [total([array[d * size : (d + 1) * size] for array in half]) for half in halves]
        for d in range(grps)
    ]

    def send(array, name, offset):
        return swap(array.astype(jnp.bfloat16), name, offset).astype(jnp.float32)

    if grps == 4:
        left, right = send(sums[3][0], "grp", 1), send(sums[3][1], "grp", 2)
        sums[2][0] += left
        sums[1][1] += right
        del sums[3]
    sums = [jnp.concatenate(pair, axis=1) for pair in sums]
    rows_sum = total([sums[0]] + [send(sums[d], "grp", d) for d in range(1, len(sums))])
    parts = [rows_sum[:, j * part_cols : (j + 1) * part_cols] for j in range(tps)]
    mixed = total([parts[0]] + [send(parts[j], "tp", j) for j in range(1, tps)])
    hidden_part = resid_in.astype(jnp.float32) + attended.astype(jnp.float32)
    return (hidden_part + mixed).astype(jnp.bfloat16)


def solution(mesh):
    return jax.shard_map(
        on_device,
        mesh=mesh,
        in_specs=(
            P(("sec", "grp"), "tp"),
            P(("sec", "grp"), "tp"),
            P(("sec", "grp"), None, "tp"),
            P(("sec", "grp"), None, None, "tp"),
            P(("sec", "grp")),
            P(),
            P(),
            P(("sec", "grp"), None),
            P("grp", None, ("sec", "tp")),
            P("grp", None, ("sec", "tp")),
            P("grp", ("sec", "tp"), None),
        ),
        out_specs=P(("sec", "grp"), "tp"),
        check_vma=False,
    )
```

```python
import functools
import math

import jax
import jax.numpy as jnp
from jax import lax
from jax.experimental import pallas as pl
from jax.experimental.pallas import tpu as pltpu
from jax.sharding import PartitionSpec as P

HEAD_DIM = 128
ROWS_STEP = 8
MIB = 1 << 20
VMEM_GATE_UP = 22

epsilon = 1e-05


def largest_divisor(total, choices):
    return next(c for c in choices if total % c == 0)


def attend_kernel(
    lengths_hbm, query_hbm, new_hbm, resid_hbm, cache_hbm, *rest, extras, kv_local, group
):
    extra_hbm, rest = rest[:extras], rest[extras:]
    (attended_ref, hidden_ref), extra_refs, rest = rest[:2], rest[2 : 2 + extras], rest[2 + extras :]
    lengths_ref, query_ref, new_ref, resid_ref, cache_ref, query_buf, output_buf, *sems = rest
    small_sem, cache_sem, extra_sem = sems
    rows = ROWS_STEP
    blocks = query_ref.shape[0] // rows
    cache_len = cache_ref.shape[2]
    stacked = group * rows
    factor = 1.0 / math.sqrt(HEAD_DIM)

    def cache_copy(b, kind):
        span = pl.ds(b * rows, rows)
        return pltpu.make_async_copy(
            cache_hbm.at[span, kind], cache_ref.at[span, kind], cache_sem.at[kind, b]
        )

    pairs = ((query_hbm, query_ref), (lengths_hbm, lengths_ref), (new_hbm, new_ref), (resid_hbm, resid_ref))
    small = [pltpu.make_async_copy(*pair, small_sem.at[i]) for i, pair in enumerate(pairs)]
    later = [
        pltpu.make_async_copy(*pair, extra_sem.at[i]) for i, pair in enumerate(zip(extra_hbm, extra_refs))
    ]
    for copy in small:
        copy.start()
    for b in range(blocks):
        for kind in range(2):
            cache_copy(b, kind).start()
    for copy in later:
        copy.start()
    small[0].wait()
    for head in range(kv_local):
        for b in range(blocks):
            query_buf[head, b] = jnp.concatenate(
                [
                    query_ref[pl.ds(b * rows, rows), pl.ds((head * group + g) * HEAD_DIM, HEAD_DIM)]
                    for g in range(group)
                ],
                axis=0,
            )
    row_of = lax.broadcasted_iota(jnp.int32, (stacked, 1), 0) % rows

    def lanes_of(head):
        return pl.ds(head * HEAD_DIM, HEAD_DIM)

    def block(b, carry):
        span = pl.ds(pl.multiple_of(b * rows, rows), rows)
        length_col = jnp.zeros((stacked, 1), jnp.int32)
        for n in range(rows):
            length_col = jnp.where(row_of == n, lengths_ref[b * rows + n], length_col)
        valid = lax.broadcasted_iota(jnp.int32, (stacked, cache_len), 1) < length_col
        cache_copy(b, 0).wait()
        scores = []
        for head in range(kv_local):
            query = query_buf[head, b]
            total = jnp.zeros((stacked, cache_len), jnp.float32)
            for n in range(rows):
                full = lax.dot_general(
                    query,
                    cache_ref[b * rows + n, 0, :, lanes_of(head)],
                    (((1,), (1,)), ((), ())),
                    preferred_element_type=jnp.float32,
                )
                total = jnp.where(row_of == n, full, total)
            scores.append(jnp.where(valid, total * factor, -jnp.inf))
        chances = []
        for head in range(kv_local):
            new_key = new_ref[span, 0, lanes_of(head)].astype(jnp.float32)
            query = query_buf[head, b].astype(jnp.float32)
            fresh = (
                jnp.sum(query * jnp.concatenate([new_key] * group, axis=0), axis=1, keepdims=True) * factor
            )
            largest = jnp.maximum(jnp.max(scores[head], axis=1, keepdims=True), fresh)
            weights = jnp.exp(scores[head] - largest)
            fresh_weight = jnp.exp(fresh - largest)
            denominator = jnp.sum(weights, axis=1, keepdims=True) + fresh_weight
            probabilities = (weights / denominator).astype(jnp.bfloat16)
            fresh_prob = (fresh_weight / denominator).astype(jnp.bfloat16).astype(jnp.float32)
            chances.append((probabilities, fresh_prob))
        cache_copy(b, 1).wait()
        for head in range(kv_local):
            probabilities, fresh_prob = chances[head]
            new_value = new_ref[span, 1, lanes_of(head)].astype(jnp.float32)
            output = jnp.zeros((stacked, HEAD_DIM), jnp.float32)
            for n in range(rows):
                full = jnp.dot(
                    probabilities,
                    cache_ref[b * rows + n, 1, :, lanes_of(head)],
                    preferred_element_type=jnp.float32,
                )
                output = jnp.where(row_of == n, full, output)
            output_buf[head, b] = output + fresh_prob * jnp.concatenate([new_value] * group, axis=0)
        return carry

    for copy in small[1:]:
        copy.wait()
    lax.fori_loop(0, blocks, block, 0)
    for head in range(kv_local):
        for g in range(group):
            columns = pl.ds((head * group + g) * HEAD_DIM, HEAD_DIM)
            piece = jnp.concatenate(
                [output_buf[head, b, pl.ds(g * rows, rows)] for b in range(blocks)], axis=0
            ).astype(jnp.bfloat16)
            attended_ref[:, columns] = piece
            hidden_ref[:, columns] = (
                resid_ref[:, columns].astype(jnp.float32) + piece.astype(jnp.float32)
            ).astype(jnp.bfloat16)
    for copy in later:
        copy.wait()


def attend(lengths, queries, new_kv, resid_in, cache, extra):
    sequences, part_cols = queries.shape
    cache_len, kv_cols = cache.shape[2:]
    kv_local = kv_cols // HEAD_DIM
    group = part_cols // kv_cols
    blocks = sequences // ROWS_STEP
    stacked = group * ROWS_STEP
    hbm = pl.BlockSpec(memory_space=pltpu.HBM)
    vmem = pl.BlockSpec(memory_space=pltpu.VMEM)
    far = [pin(a, pltpu.HBM) for a in (lengths, queries, new_kv, resid_in, cache, *extra)]
    return pl.pallas_call(
        functools.partial(attend_kernel, extras=len(extra), kv_local=kv_local, group=group),
        in_specs=[hbm] * len(far),
        out_specs=[vmem] * (2 + len(extra)),
        out_shape=[pltpu.VMEM((sequences, part_cols), jnp.bfloat16)] * 2
        + [pltpu.VMEM(array.shape, array.dtype) for array in extra],
        scratch_shapes=[
            pltpu.SMEM(lengths.shape, lengths.dtype),
            pltpu.VMEM(queries.shape, queries.dtype),
            pltpu.VMEM(new_kv.shape, new_kv.dtype),
            pltpu.VMEM(resid_in.shape, resid_in.dtype),
            pltpu.VMEM(cache.shape, cache.dtype),
            pltpu.VMEM((kv_local, blocks, stacked, HEAD_DIM), jnp.bfloat16),
            pltpu.VMEM((kv_local, blocks, stacked, HEAD_DIM), jnp.float32),
            pltpu.SemaphoreType.DMA((4,)),
            pltpu.SemaphoreType.DMA((2, blocks)),
            pltpu.SemaphoreType.DMA((len(extra),)),
        ],
        cost_estimate=pl.CostEstimate(
            flops=0, bytes_accessed=2 * cache.size, transcendentals=0
        ),
        compiler_params=pltpu.CompilerParams(vmem_limit_bytes=16 * MIB),
        name="attend",
    )(*far)


def fetch_kernel(after_ref, earlier_ref, source_hbm, target_ref, token_ref, sem, *, index, first):
    pieces = sem.shape[0]
    step = target_ref.shape[0] // pieces
    copies = [
        pltpu.make_async_copy(
            source_hbm.at[index, pl.ds(first + i * step, step)],
            target_ref.at[pl.ds(i * step, step)],
            sem.at[i],
        )
        for i in range(pieces)
    ]
    for copy in copies:
        copy.start()
    token_ref[...] = jnp.zeros_like(token_ref)
    for copy in copies:
        copy.wait()


def fetch(after, earlier, weights, index, first, rows):
    shape = (rows, weights.shape[2])
    pieces = 4
    return pl.pallas_call(
        functools.partial(fetch_kernel, index=index, first=first),
        in_specs=[pl.BlockSpec(memory_space=pl.ANY)] * 2 + [pl.BlockSpec(memory_space=pltpu.HBM)],
        out_specs=[pl.BlockSpec(memory_space=pltpu.VMEM)] * 2,
        out_shape=[pltpu.VMEM(shape, weights.dtype), pltpu.VMEM((8, 128), jnp.float32)],
        scratch_shapes=[pltpu.SemaphoreType.DMA((pieces,))],
        cost_estimate=pl.CostEstimate(flops=0, bytes_accessed=2 * math.prod(shape), transcendentals=0),
        compiler_params=pltpu.CompilerParams(vmem_limit_bytes=1 * MIB),
        name="fetch",
    )(after, earlier, pin(weights, pltpu.HBM))


def norm_kernel(gain_ref, router_ref, ids_ref, *rest):
    part_refs, own_ref = rest[:-1], rest[-1]
    tps = len(part_refs)
    rows, part_cols = part_refs[0].shape
    width = tps * part_cols
    experts = router_ref.shape[0]
    tp = lax.axis_index("tp")
    places = [pl.ds(pl.multiple_of((j ^ tp) * part_cols, 128), part_cols) for j in range(tps)]
    raws = [ref[...].astype(jnp.float32) for ref in part_refs]
    squares = sum(jnp.sum(raw * raw, axis=1, keepdims=True) for raw in raws)
    row_scale = lax.rsqrt(squares / width + epsilon)
    logits = jnp.zeros((rows, 2 * experts), jnp.float32)
    for raw, there in zip(raws, places):
        normed = (raw * row_scale * gain_ref[:, there]).astype(jnp.bfloat16)
        own_ref[:, there] = normed
        router = router_ref[:, there]
        high = router.astype(jnp.bfloat16).astype(jnp.float32)
        both = jnp.concatenate([high, router - high], axis=0).astype(jnp.bfloat16)
        logits += lax.dot_general(
            normed, both, (((1,), (1,)), ((), ())), preferred_element_type=jnp.float32
        )
    logits = logits[:, :experts] + logits[:, experts:]
    square = [lax.broadcasted_iota(jnp.int32, (rows, rows), axis) for axis in range(2)]
    identity = jnp.where(square[0] == square[1], 1.0, 0.0)
    ids = lax.dot_general(
        identity, ids_ref[...].astype(jnp.float32), (((1,), (1,)), ((), ())), preferred_element_type=jnp.float32
    ).astype(jnp.int32)
    names = [ids[:, k : k + 1] for k in range(2)]
    lane = lax.broadcasted_iota(jnp.int32, (rows, experts), 1)
    picked = [jnp.sum(jnp.where(lane == name, logits, 0.0), axis=1, keepdims=True) for name in names]
    mixes = [
        1.0 / (1.0 + jnp.exp(picked[1] - picked[0])),
        1.0 / (1.0 + jnp.exp(picked[0] - picked[1])),
    ]
    lane = lax.broadcasted_iota(jnp.int32, (rows, 128), 1)
    share = sum(jnp.where(lane % experts == name, mix, 0.0) for name, mix in zip(names, mixes))
    high = share.astype(jnp.bfloat16).astype(jnp.float32)
    own_ref[:, pl.ds(width, 128)] = jnp.where(lane < experts, high, share - high).astype(jnp.bfloat16)


def norm(gain, router, route_ids, parts):
    rows, part_cols = parts[0].shape
    vmem = pl.BlockSpec(memory_space=pltpu.VMEM)
    near = [pin(a, pltpu.VMEM) for a in (gain, router, route_ids, *parts)]
    return pl.pallas_call(
        norm_kernel,
        in_specs=[vmem] * len(near),
        out_specs=vmem,
        out_shape=pltpu.VMEM((rows, part_cols * len(parts) + 128), jnp.bfloat16),
        compiler_params=pltpu.CompilerParams(vmem_limit_bytes=2 * MIB),
        name="norm",
    )(*near)


def split_kernel(first_ref, second_ref, left_ref, right_ref):
    cut = left_ref.shape[1]
    left_ref[...] = first_ref[:, pl.ds(0, cut)]
    right_ref[...] = second_ref[:, pl.ds(cut, right_ref.shape[1])]


def split(first, second, cut):
    rows, width = first.shape
    vmem = pl.BlockSpec(memory_space=pltpu.VMEM)
    return pl.pallas_call(
        split_kernel,
        in_specs=[vmem] * 2,
        out_specs=[vmem] * 2,
        out_shape=[pltpu.VMEM((rows, cut), first.dtype), pltpu.VMEM((rows, width - cut), first.dtype)],
        compiler_params=pltpu.CompilerParams(vmem_limit_bytes=1 * MIB),
        name="split",
    )(pin(first, pltpu.VMEM), pin(second, pltpu.VMEM))


def gate_up_kernel(gate_hbm, up_hbm, token_ref, gate_ref, *rest, layout, experts, blocks_held, depth, nb):
    pieces = sum(layout)
    piece_refs, (act_ref, buf, rows_ref, sem) = rest[:pieces], rest[pieces:]
    held, width, ff = gate_hbm.shape
    ready = 1
    blocks = ff // nb
    deep = buf.shape[1]
    cuts = width // deep
    steps = (2 * held - ready) * blocks * cuts
    grp = lax.axis_index("grp")

    def block_copy(hbm, e, n, i):
        slot = lax.rem(i, depth)
        columns = pl.ds(pl.multiple_of(n * nb, 128), nb)
        there = pl.ds(pl.multiple_of(i % cuts * deep, 128), deep)
        return pltpu.make_async_copy(hbm.at[e, there, columns], buf.at[slot], sem.at[slot])

    def start(i):
        first = 0
        for e in range(held):
            kinds = (up_hbm,) if e < ready else (gate_hbm, up_hbm)
            for which, hbm in enumerate(kinds):
                inside = i // cuts - first
                hit = (inside >= 0) & (inside < len(kinds) * blocks) & (inside % len(kinds) == which)

                @pl.when(hit)
                def _():
                    block_copy(hbm, e, inside // len(kinds), i).start()

            first += len(kinds) * blocks

    def prime(i, carry):
        start(i)
        return carry

    lax.fori_loop(0, min(depth, steps), prime, 0)

    rows_of, first = [], 0
    for parts in layout:
        rows_of.append(piece_refs[first : first + parts])
        first += parts

    def gather(start_column, size):
        found = []
        for refs in rows_of:
            at = start_column
            for ref in refs:
                if at < ref.shape[1]:
                    found.append(ref[:, pl.ds(at, size)].astype(jnp.float32))
                    break
                at -= ref.shape[1]
        return jnp.concatenate(found, axis=0)

    for k in range(width // deep):
        rows_ref[:, pl.ds(k * deep, deep)] = gather(k * deep, deep).astype(jnp.bfloat16)
    shares = gather(width, 128)
    shares = shares[:, :experts] + shares[:, experts : 2 * experts]
    lane = lax.broadcasted_iota(jnp.int32, shares.shape, 1)

    def streamed(block):
        product = 0.0
        for cut in range(cuts):
            i = block * cuts + cut
            block_copy(gate_hbm, 0, 0, i).wait()
            there = pl.ds(cut * deep, deep)
            product += jnp.dot(
                rows_ref[:, there], buf[lax.rem(i, depth)], preferred_element_type=jnp.float32
            )

            @pl.when(i + depth < steps)
            def _():
                start(i + depth)

        return product

    first = 0
    for e in range(held):
        expert = (grp * held + e) // blocks_held
        share = jnp.sum(jnp.where(lane == expert, shares, 0.0), axis=1, keepdims=True)

        def body(n, carry, e=e, first=first, share=share):
            columns = pl.ds(pl.multiple_of(n * nb, 128), nb)
            if e < ready:
                i = first + n
                gate = jnp.dot(rows_ref[...], gate_ref[:, columns], preferred_element_type=jnp.float32)
            else:
                i = first + 2 * n + 1
                gate = streamed(i - 1)
            up = streamed(i) * share
            out = pl.ds(pl.multiple_of(e * ff + n * nb, 128), nb)
            act_ref[:, out] = (gate / (1.0 + jnp.exp(-gate)) * up).astype(jnp.bfloat16)
            return carry

        lax.fori_loop(0, blocks, body, 0)
        first += (1 if e < ready else 2) * blocks


def gate_up(w_gate, w_up, token, gate_ready, pieces, experts, blocks_held):
    held, width, ff = w_gate.shape
    tokens = sum(parts[0].shape[0] for parts in pieces)
    nb = largest_divisor(ff, (1024, 512, 256, 128))
    depth, cuts = 4, 4
    vmem = pl.BlockSpec(memory_space=pltpu.VMEM)
    hbm = pl.BlockSpec(memory_space=pltpu.HBM)
    near = [pin(a, pltpu.VMEM) for a in (gate_ready, *(part for parts in pieces for part in parts))]
    return pl.pallas_call(
        functools.partial(
            gate_up_kernel,
            layout=tuple(len(parts) for parts in pieces),
            experts=experts,
            blocks_held=blocks_held,
            depth=depth,
            nb=nb,
        ),
        in_specs=[hbm] * 2 + [pl.BlockSpec(memory_space=pl.ANY)] + [vmem] * len(near),
        out_specs=vmem,
        out_shape=pltpu.VMEM((tokens, held * ff), jnp.bfloat16),
        scratch_shapes=[
            pltpu.VMEM((depth, width // cuts, nb), jnp.bfloat16),
            pltpu.VMEM((tokens, width), jnp.bfloat16),
            pltpu.SemaphoreType.DMA((depth,)),
        ],
        cost_estimate=pl.CostEstimate(
            flops=4 * held * tokens * width * ff, bytes_accessed=4 * held * width * ff, transcendentals=0
        ),
        compiler_params=pltpu.CompilerParams(vmem_limit_bytes=VMEM_GATE_UP * MIB),
        name="gate_up",
    )(pin(w_gate, pltpu.HBM), pin(w_up, pltpu.HBM), token, *near)


def down_kernel(act_ref, *rest, first, part_cols, cuts):
    down_refs, (own_ref, other_ref) = rest[:-2], rest[-2:]
    starts = [sum(ref.shape[0] for ref in down_refs[:i]) for i in range(len(down_refs))]
    half = own_ref.shape[0]
    nb = part_cols // cuts
    tp = lax.axis_index("tp")

    def body(i, carry):
        j = first + i // cuts
        there = pl.ds(pl.multiple_of((j ^ tp) * part_cols + i % cuts * nb, 128), nb)
        partial = sum(
            jnp.dot(
                act_ref[:, pl.ds(start, ref.shape[0])], ref[:, there], preferred_element_type=jnp.float32
            )
            for start, ref in zip(starts, down_refs)
        )
        columns = pl.ds(pl.multiple_of(i * nb, 128), nb)
        own_ref[:, columns] = partial[:half].astype(jnp.bfloat16)
        other_ref[:, columns] = partial[half:].astype(jnp.bfloat16)
        return carry

    lax.fori_loop(0, own_ref.shape[1] // nb, body, 0)


def down(act, weights, first, parts, part_cols, secs):
    tokens, depth = act.shape
    vmem = pl.BlockSpec(memory_space=pltpu.VMEM)
    near = [pin(a, pltpu.VMEM) for a in (act, *weights)]
    return pl.pallas_call(
        functools.partial(down_kernel, first=first, part_cols=part_cols, cuts=2),
        in_specs=[vmem] * len(near),
        out_specs=[vmem] * secs,
        out_shape=[pltpu.VMEM((tokens // secs, parts * part_cols), jnp.bfloat16)] * secs,
        cost_estimate=pl.CostEstimate(
            flops=2 * tokens * depth * parts * part_cols, bytes_accessed=0, transcendentals=0
        ),
        compiler_params=pltpu.CompilerParams(vmem_limit_bytes=4 * MIB),
        name="down",
    )(*near)


def pin(array, space):
    return pltpu.with_memory_space_constraint(array, space)


def swap(array, axis, offset):
    size = lax.axis_size(axis)
    return lax.ppermute(array, axis, [(i, i ^ offset) for i in range(size)])


def on_device(
    resid_in, queries, new_kv, cache, lengths, norm_gain, router, route_ids, w_gate, w_up, w_down
):
    sequences, part_cols = resid_in.shape
    tps, grps, secs = lax.axis_size("tp"), lax.axis_size("grp"), lax.axis_size("sec")
    held = w_gate.shape[0]
    blocks_held = max(1, grps * held // router.shape[1])
    tie = lax.optimization_barrier
    attended, hidden, gain, router_rows, ids = attend(
        lengths, queries, new_kv, resid_in, cache, (norm_gain.reshape(1, -1), router.T, route_ids.T)
    )

    ff = w_down.shape[1]
    spans = [(e, 0, ff) for e in range(held - 1)]
    spans += [(held - 1, 0, ff // 4), (held - 1, ff // 4, ff - ff // 4)]
    down_ready = []

    def fetch_down(after, token, count):
        for e, first, rows in spans[len(down_ready) : len(down_ready) + count]:
            ready, token = fetch(after, token, w_down, e, first, rows)
            down_ready.append(ready)
        return token

    parts = [hidden] + [swap(hidden, "tp", j) for j in range(1, tps)]
    gate_ready, token = fetch(hidden, hidden, w_gate, 0, 0, w_gate.shape[1])
    parts, token = tie((parts, token))
    own = norm(gain, router_rows, ids, parts)
    if grps == 4:
        near = [own, swap(own, "grp", 1), swap(own, "grp", 2)]
        token = fetch_down(own, token, len(spans) - 1)
        near, token = tie((near, token))
        after, right = split(near[2], near[1], tps // 2 * part_cols)
        across = [swap(after, "grp", 1), swap(right, "grp", 2)]
        near = [[array] for array in near]
    else:
        near = [[own]] + [[swap(own, "grp", d)] for d in range(1, grps - 1)]
        after = own
        across = [swap(own, "grp", grps - 1)]
    token = fetch_down(after, token, len(spans))
    across, token = tie((across, token))
    near.append(across)
    pieces = near + [[swap(array, "sec", 1) for array in arrays] for arrays in near]
    act = gate_up(w_gate, w_up, token, gate_ready, pieces, router.shape[1], blocks_held)

    def total(arrays):
        result = arrays[0].astype(jnp.float32)
        for array in arrays[1:]:
            result = result + array.astype(jnp.float32)
        return result

    halves = []
    for c in range(2):
        kept, sent = down(act, down_ready, c * tps // 2, tps // 2, part_cols, secs)
        act, _ = tie((act, sent))
        halves.append((kept, swap(sent, "sec", 1)))
    size = sequences
    sums = [
        [total([array[d * size : (d + 1) * size] for array in half]) for half in halves]
        for d in range(grps)
    ]

    def send(array, name, offset):
        return swap(array.astype(jnp.bfloat16), name, offset).astype(jnp.float32)

    if grps == 4:
        left, right = send(sums[3][0], "grp", 1), send(sums[3][1], "grp", 2)
        sums[2][0] += left
        sums[1][1] += right
        del sums[3]
    sums = [jnp.concatenate(pair, axis=1) for pair in sums]
    rows_sum = total([sums[0]] + [send(sums[d], "grp", d) for d in range(1, len(sums))])
    parts = [rows_sum[:, j * part_cols : (j + 1) * part_cols] for j in range(tps)]
    mixed = total([parts[0]] + [send(parts[j], "tp", j) for j in range(1, tps)])
    hidden_part = resid_in.astype(jnp.float32) + attended.astype(jnp.float32)
    return (hidden_part + mixed).astype(jnp.bfloat16)


def solution(mesh):
    return jax.shard_map(
        on_device,
        mesh=mesh,
        in_specs=(
            P(("sec", "grp"), "tp"),
            P(("sec", "grp"), "tp"),
            P(("sec", "grp"), None, "tp"),
            P(("sec", "grp"), None, None, "tp"),
            P(("sec", "grp")),
            P(),
            P(),
            P(("sec", "grp"), None),
            P("grp", None, ("sec", "tp")),
            P("grp", None, ("sec", "tp")),
            P("grp", ("sec", "tp"), None),
        ),
        out_specs=P(("sec", "grp"), "tp"),
        check_vma=False,
    )
```

```python
import functools
import math

import jax
import jax.numpy as jnp
from jax import lax
from jax.experimental import pallas as pl
from jax.experimental.pallas import tpu as pltpu
from jax.sharding import PartitionSpec as P

HEAD_DIM = 128
ROWS_STEP = 8
MIB = 1 << 20
VMEM_GATE_UP = 22

epsilon = 1e-05


def largest_divisor(total, choices):
    return next(c for c in choices if total % c == 0)


def attend_kernel(
    lengths_hbm, query_hbm, new_hbm, resid_hbm, cache_hbm, *rest, extras, kv_local, group
):
    extra_hbm, rest = rest[:extras], rest[extras:]
    (attended_ref, hidden_ref), extra_refs, rest = rest[:2], rest[2 : 2 + extras], rest[2 + extras :]
    lengths_ref, query_ref, new_ref, resid_ref, cache_ref, query_buf, output_buf, *sems = rest
    small_sem, cache_sem, extra_sem = sems
    rows = ROWS_STEP
    blocks = query_ref.shape[0] // rows
    cache_len = cache_ref.shape[2]
    stacked = group * rows
    factor = 1.0 / math.sqrt(HEAD_DIM)

    def cache_copy(b, kind):
        span = pl.ds(b * rows, rows)
        return pltpu.make_async_copy(
            cache_hbm.at[span, kind], cache_ref.at[span, kind], cache_sem.at[kind, b]
        )

    pairs = ((query_hbm, query_ref), (lengths_hbm, lengths_ref), (new_hbm, new_ref), (resid_hbm, resid_ref))
    small = [pltpu.make_async_copy(*pair, small_sem.at[i]) for i, pair in enumerate(pairs)]
    later = [
        pltpu.make_async_copy(*pair, extra_sem.at[i]) for i, pair in enumerate(zip(extra_hbm, extra_refs))
    ]
    for copy in small:
        copy.start()
    for b in range(blocks):
        for kind in range(2):
            cache_copy(b, kind).start()
    for copy in later:
        copy.start()
    small[0].wait()
    for head in range(kv_local):
        for b in range(blocks):
            query_buf[head, b] = jnp.concatenate(
                [
                    query_ref[pl.ds(b * rows, rows), pl.ds((head * group + g) * HEAD_DIM, HEAD_DIM)]
                    for g in range(group)
                ],
                axis=0,
            )
    row_of = lax.broadcasted_iota(jnp.int32, (stacked, 1), 0) % rows

    def lanes_of(head):
        return pl.ds(head * HEAD_DIM, HEAD_DIM)

    def block(b, carry):
        span = pl.ds(pl.multiple_of(b * rows, rows), rows)
        length_col = jnp.zeros((stacked, 1), jnp.int32)
        for n in range(rows):
            length_col = jnp.where(row_of == n, lengths_ref[b * rows + n], length_col)
        valid = lax.broadcasted_iota(jnp.int32, (stacked, cache_len), 1) < length_col
        cache_copy(b, 0).wait()
        scores = []
        for head in range(kv_local):
            query = query_buf[head, b]
            total = jnp.zeros((stacked, cache_len), jnp.float32)
            for n in range(rows):
                full = lax.dot_general(
                    query,
                    cache_ref[b * rows + n, 0, :, lanes_of(head)],
                    (((1,), (1,)), ((), ())),
                    preferred_element_type=jnp.float32,
                )
                total = jnp.where(row_of == n, full, total)
            scores.append(jnp.where(valid, total * factor, -jnp.inf))
        chances = []
        for head in range(kv_local):
            new_key = new_ref[span, 0, lanes_of(head)].astype(jnp.float32)
            query = query_buf[head, b].astype(jnp.float32)
            fresh = (
                jnp.sum(query * jnp.concatenate([new_key] * group, axis=0), axis=1, keepdims=True) * factor
            )
            largest = jnp.maximum(jnp.max(scores[head], axis=1, keepdims=True), fresh)
            weights = jnp.exp(scores[head] - largest)
            fresh_weight = jnp.exp(fresh - largest)
            denominator = jnp.sum(weights, axis=1, keepdims=True) + fresh_weight
            probabilities = (weights / denominator).astype(jnp.bfloat16)
            fresh_prob = (fresh_weight / denominator).astype(jnp.bfloat16).astype(jnp.float32)
            chances.append((probabilities, fresh_prob))
        cache_copy(b, 1).wait()
        for head in range(kv_local):
            probabilities, fresh_prob = chances[head]
            new_value = new_ref[span, 1, lanes_of(head)].astype(jnp.float32)
            output = jnp.zeros((stacked, HEAD_DIM), jnp.float32)
            for n in range(rows):
                full = jnp.dot(
                    probabilities,
                    cache_ref[b * rows + n, 1, :, lanes_of(head)],
                    preferred_element_type=jnp.float32,
                )
                output = jnp.where(row_of == n, full, output)
            output_buf[head, b] = output + fresh_prob * jnp.concatenate([new_value] * group, axis=0)
        return carry

    for copy in small[1:]:
        copy.wait()
    lax.fori_loop(0, blocks, block, 0)
    for head in range(kv_local):
        for g in range(group):
            columns = pl.ds((head * group + g) * HEAD_DIM, HEAD_DIM)
            piece = jnp.concatenate(
                [output_buf[head, b, pl.ds(g * rows, rows)] for b in range(blocks)], axis=0
            ).astype(jnp.bfloat16)
            attended_ref[:, columns] = piece
            hidden_ref[:, columns] = (
                resid_ref[:, columns].astype(jnp.float32) + piece.astype(jnp.float32)
            ).astype(jnp.bfloat16)
    for copy in later:
        copy.wait()


def attend(lengths, queries, new_kv, resid_in, cache, extra):
    sequences, part_cols = queries.shape
    cache_len, kv_cols = cache.shape[2:]
    kv_local = kv_cols // HEAD_DIM
    group = part_cols // kv_cols
    blocks = sequences // ROWS_STEP
    stacked = group * ROWS_STEP
    hbm = pl.BlockSpec(memory_space=pltpu.HBM)
    vmem = pl.BlockSpec(memory_space=pltpu.VMEM)
    far = [pin(a, pltpu.HBM) for a in (lengths, queries, new_kv, resid_in, cache, *extra)]
    return pl.pallas_call(
        functools.partial(attend_kernel, extras=len(extra), kv_local=kv_local, group=group),
        in_specs=[hbm] * len(far),
        out_specs=[vmem] * (2 + len(extra)),
        out_shape=[pltpu.VMEM((sequences, part_cols), jnp.bfloat16)] * 2
        + [pltpu.VMEM(array.shape, array.dtype) for array in extra],
        scratch_shapes=[
            pltpu.SMEM(lengths.shape, lengths.dtype),
            pltpu.VMEM(queries.shape, queries.dtype),
            pltpu.VMEM(new_kv.shape, new_kv.dtype),
            pltpu.VMEM(resid_in.shape, resid_in.dtype),
            pltpu.VMEM(cache.shape, cache.dtype),
            pltpu.VMEM((kv_local, blocks, stacked, HEAD_DIM), jnp.bfloat16),
            pltpu.VMEM((kv_local, blocks, stacked, HEAD_DIM), jnp.float32),
            pltpu.SemaphoreType.DMA((4,)),
            pltpu.SemaphoreType.DMA((2, blocks)),
            pltpu.SemaphoreType.DMA((len(extra),)),
        ],
        cost_estimate=pl.CostEstimate(
            flops=0, bytes_accessed=2 * cache.size, transcendentals=0
        ),
        compiler_params=pltpu.CompilerParams(vmem_limit_bytes=16 * MIB),
        name="attend",
    )(*far)


def span_copies(source_hbm, targets, sems, spans, first, part_cols):
    tp = lax.axis_index("tp")
    copies = []
    for (e, row), target, sem in zip(spans, targets, sems):
        rows, width = target.shape
        pieces = sem.shape[0]
        for i in range(pieces):
            if part_cols:
                there = pl.ds(pl.multiple_of((first + i ^ tp) * part_cols, 128), part_cols)
                source, here = source_hbm.at[e, pl.ds(row, rows), there], (slice(None), pl.ds(i * part_cols, part_cols))
            else:
                step = rows // pieces
                source, here = source_hbm.at[e, pl.ds(row + i * step, step)], (pl.ds(i * step, step),)
            copies.append(pltpu.make_async_copy(source, target.at[here], sem.at[i]))
    return copies


def fetch_kernel(after_ref, earlier_ref, *rest, jobs):
    sources, rest = rest[: len(jobs)], rest[len(jobs) :]
    count = sum(len(spans) for spans, _ in jobs)
    targets, token_ref, sems = rest[:count], rest[count], rest[count + 1 :]
    copies, at = [], 0
    for source, (spans, part_cols) in zip(sources, jobs):
        here = slice(at, at + len(spans))
        copies += span_copies(source, targets[here], sems[here], spans, 0, part_cols)
        at += len(spans)
    for copy in copies:
        copy.start()
    token_ref[...] = jnp.zeros_like(token_ref)
    for copy in copies:
        copy.wait()


def fetch(after, earlier, jobs):
    shapes, parts_of = [], []
    for weights, spans, parts, part_cols in jobs:
        for _, _, rows in spans:
            shapes.append((rows, parts * part_cols if parts else weights.shape[2]))
            parts_of.append(parts or 4)
    size = sum(math.prod(shape) for shape in shapes)
    return pl.pallas_call(
        functools.partial(
            fetch_kernel,
            jobs=[([span[:2] for span in spans], part_cols) for _, spans, _, part_cols in jobs],
        ),
        in_specs=[pl.BlockSpec(memory_space=pl.ANY)] * 2 + [pl.BlockSpec(memory_space=pltpu.HBM)] * len(jobs),
        out_specs=[pl.BlockSpec(memory_space=pltpu.VMEM)] * (len(shapes) + 1),
        out_shape=[pltpu.VMEM(shape, jnp.bfloat16) for shape in shapes] + [pltpu.VMEM((8, 128), jnp.float32)],
        scratch_shapes=[pltpu.SemaphoreType.DMA((parts,)) for parts in parts_of],
        cost_estimate=pl.CostEstimate(flops=0, bytes_accessed=2 * size, transcendentals=0),
        compiler_params=pltpu.CompilerParams(vmem_limit_bytes=1 * MIB),
        name="fetch",
    )(after, earlier, *(pin(job[0], pltpu.HBM) for job in jobs))


def norm_kernel(gain_ref, router_ref, ids_ref, *rest):
    part_refs, own_ref = rest[:-1], rest[-1]
    tps = len(part_refs)
    rows, part_cols = part_refs[0].shape
    width = tps * part_cols
    experts = router_ref.shape[0]
    tp = lax.axis_index("tp")
    places = [pl.ds(pl.multiple_of((j ^ tp) * part_cols, 128), part_cols) for j in range(tps)]
    raws = [ref[...].astype(jnp.float32) for ref in part_refs]
    squares = sum(jnp.sum(raw * raw, axis=1, keepdims=True) for raw in raws)
    row_scale = lax.rsqrt(squares / width + epsilon)
    logits = jnp.zeros((rows, 2 * experts), jnp.float32)
    for raw, there in zip(raws, places):
        normed = (raw * row_scale * gain_ref[:, there]).astype(jnp.bfloat16)
        own_ref[:, there] = normed
        router = router_ref[:, there]
        high = router.astype(jnp.bfloat16).astype(jnp.float32)
        both = jnp.concatenate([high, router - high], axis=0).astype(jnp.bfloat16)
        logits += lax.dot_general(
            normed, both, (((1,), (1,)), ((), ())), preferred_element_type=jnp.float32
        )
    logits = logits[:, :experts] + logits[:, experts:]
    square = [lax.broadcasted_iota(jnp.int32, (rows, rows), axis) for axis in range(2)]
    identity = jnp.where(square[0] == square[1], 1.0, 0.0)
    ids = lax.dot_general(
        identity, ids_ref[...].astype(jnp.float32), (((1,), (1,)), ((), ())), preferred_element_type=jnp.float32
    ).astype(jnp.int32)
    names = [ids[:, k : k + 1] for k in range(2)]
    lane = lax.broadcasted_iota(jnp.int32, (rows, experts), 1)
    picked = [jnp.sum(jnp.where(lane == name, logits, 0.0), axis=1, keepdims=True) for name in names]
    mixes = [
        1.0 / (1.0 + jnp.exp(picked[1] - picked[0])),
        1.0 / (1.0 + jnp.exp(picked[0] - picked[1])),
    ]
    lane = lax.broadcasted_iota(jnp.int32, (rows, 128), 1)
    share = sum(jnp.where(lane % experts == name, mix, 0.0) for name, mix in zip(names, mixes))
    high = share.astype(jnp.bfloat16).astype(jnp.float32)
    own_ref[:, pl.ds(width, 128)] = jnp.where(lane < experts, high, share - high).astype(jnp.bfloat16)


def norm(gain, router, route_ids, parts):
    rows, part_cols = parts[0].shape
    vmem = pl.BlockSpec(memory_space=pltpu.VMEM)
    near = [pin(a, pltpu.VMEM) for a in (gain, router, route_ids, *parts)]
    return pl.pallas_call(
        norm_kernel,
        in_specs=[vmem] * len(near),
        out_specs=vmem,
        out_shape=pltpu.VMEM((rows, part_cols * len(parts) + 128), jnp.bfloat16),
        compiler_params=pltpu.CompilerParams(vmem_limit_bytes=2 * MIB),
        name="norm",
    )(*near)


def split_kernel(first_ref, second_ref, left_ref, right_ref):
    cut = left_ref.shape[1]
    left_ref[...] = first_ref[:, pl.ds(0, cut)]
    right_ref[...] = second_ref[:, pl.ds(cut, right_ref.shape[1])]


def split(first, second, cut):
    rows, width = first.shape
    vmem = pl.BlockSpec(memory_space=pltpu.VMEM)
    return pl.pallas_call(
        split_kernel,
        in_specs=[vmem] * 2,
        out_specs=[vmem] * 2,
        out_shape=[pltpu.VMEM((rows, cut), first.dtype), pltpu.VMEM((rows, width - cut), first.dtype)],
        compiler_params=pltpu.CompilerParams(vmem_limit_bytes=1 * MIB),
        name="split",
    )(pin(first, pltpu.VMEM), pin(second, pltpu.VMEM))


def gate_up_kernel(gate_hbm, up_hbm, token_ref, gate_ref, up_ref, *rest, layout, experts, blocks_held, depth, nb):
    pieces = sum(layout)
    piece_refs, (act_ref, buf, rows_ref, sem) = rest[:pieces], rest[pieces:]
    held, width, ff = gate_hbm.shape
    ready = 1
    blocks = ff // nb
    deep = buf.shape[1]
    cuts = width // deep
    steps = (2 * held - ready) * blocks * cuts - 1
    grp = lax.axis_index("grp")

    def block_copy(hbm, e, n, i):
        slot = lax.rem(i, depth)
        columns = pl.ds(pl.multiple_of(n * nb, 128), nb)
        there = pl.ds(pl.multiple_of((i + 1) % cuts * deep, 128), deep)
        return pltpu.make_async_copy(hbm.at[e, there, columns], buf.at[slot], sem.at[slot])

    def start(i):
        first = 0
        for e in range(held):
            kinds = (up_hbm,) if e < ready else (gate_hbm, up_hbm)
            for which, hbm in enumerate(kinds):
                inside = (i + 1) // cuts - first
                hit = (inside >= 0) & (inside < len(kinds) * blocks) & (inside % len(kinds) == which)

                @pl.when(hit)
                def _():
                    block_copy(hbm, e, inside // len(kinds), i).start()

            first += len(kinds) * blocks

    def prime(i, carry):
        start(i)
        return carry

    lax.fori_loop(0, min(depth, steps), prime, 0)

    rows_of, first = [], 0
    for parts in layout:
        rows_of.append(piece_refs[first : first + parts])
        first += parts

    def gather(start_column, size):
        found = []
        for refs in rows_of:
            at = start_column
            for ref in refs:
                if at < ref.shape[1]:
                    found.append(ref[:, pl.ds(at, size)].astype(jnp.float32))
                    break
                at -= ref.shape[1]
        return jnp.concatenate(found, axis=0)

    for k in range(width // deep):
        rows_ref[:, pl.ds(k * deep, deep)] = gather(k * deep, deep).astype(jnp.bfloat16)
    shares = gather(width, 128)
    shares = shares[:, :experts] + shares[:, experts : 2 * experts]
    lane = lax.broadcasted_iota(jnp.int32, shares.shape, 1)

    def streamed(block, has_first=False):
        product = 0.0
        for cut in range(cuts):
            there = pl.ds(cut * deep, deep)
            if cut == 0 and has_first:
                product += jnp.dot(rows_ref[:, there], up_ref[...], preferred_element_type=jnp.float32)
                continue
            i = block * cuts + cut - 1
            block_copy(gate_hbm, 0, 0, i).wait()
            product += jnp.dot(
                rows_ref[:, there], buf[lax.rem(i, depth)], preferred_element_type=jnp.float32
            )

            @pl.when(i + depth < steps)
            def _():
                start(i + depth)

        return product

    first = 0
    for e in range(held):
        expert = (grp * held + e) // blocks_held
        share = jnp.sum(jnp.where(lane == expert, shares, 0.0), axis=1, keepdims=True)

        def body(n, carry, e=e, first=first, share=share):
            columns = pl.ds(pl.multiple_of(n * nb, 128), nb)
            if e < ready:
                i = first + n
                gate = jnp.dot(rows_ref[...], gate_ref[:, columns], preferred_element_type=jnp.float32)
            else:
                i = first + 2 * n + 1
                gate = streamed(i - 1)
            up = streamed(i, e < ready) * share
            out = pl.ds(pl.multiple_of(e * ff + n * nb, 128), nb)
            act_ref[:, out] = (gate / (1.0 + jnp.exp(-gate)) * up).astype(jnp.bfloat16)
            return carry

        lax.fori_loop(0, blocks, body, 0)
        first += (1 if e < ready else 2) * blocks


def gate_up(w_gate, w_up, token, gate_ready, up_ready, pieces, experts, blocks_held):
    held, width, ff = w_gate.shape
    tokens = sum(parts[0].shape[0] for parts in pieces)
    nb = largest_divisor(ff, (1024, 512, 256, 128))
    depth, cuts = 4, 4
    vmem = pl.BlockSpec(memory_space=pltpu.VMEM)
    hbm = pl.BlockSpec(memory_space=pltpu.HBM)
    near = [pin(a, pltpu.VMEM) for a in (gate_ready, up_ready, *(part for parts in pieces for part in parts))]
    return pl.pallas_call(
        functools.partial(
            gate_up_kernel,
            layout=tuple(len(parts) for parts in pieces),
            experts=experts,
            blocks_held=blocks_held,
            depth=depth,
            nb=nb,
        ),
        in_specs=[hbm] * 2 + [pl.BlockSpec(memory_space=pl.ANY)] + [vmem] * len(near),
        out_specs=vmem,
        out_shape=pltpu.VMEM((tokens, held * ff), jnp.bfloat16),
        scratch_shapes=[
            pltpu.VMEM((depth, width // cuts, nb), jnp.bfloat16),
            pltpu.VMEM((tokens, width), jnp.bfloat16),
            pltpu.SemaphoreType.DMA((depth,)),
        ],
        cost_estimate=pl.CostEstimate(
            flops=4 * held * tokens * width * ff, bytes_accessed=4 * held * width * ff, transcendentals=0
        ),
        compiler_params=pltpu.CompilerParams(vmem_limit_bytes=VMEM_GATE_UP * MIB),
        name="gate_up",
    )(pin(w_gate, pltpu.HBM), pin(w_up, pltpu.HBM), token, *near)


def down_kernel(act_ref, *rest, count, nb, spans, first, part_cols):
    down_refs, rest = rest[:count], rest[count:]
    if spans:
        down_hbm, own_ref, other_ref, *rest = rest
        targets, sems = rest[: len(spans)], rest[len(spans) :]
        copies = span_copies(down_hbm, targets, sems, spans, first, part_cols)
    else:
        copies, (own_ref, other_ref) = [], rest
    for copy in copies:
        copy.start()
    starts = [sum(ref.shape[0] for ref in down_refs[:i]) for i in range(count)]
    half = own_ref.shape[0]

    def body(i, carry):
        columns = pl.ds(pl.multiple_of(i * nb, 128), nb)
        partial = sum(
            jnp.dot(
                act_ref[:, pl.ds(start, ref.shape[0])], ref[:, columns], preferred_element_type=jnp.float32
            )
            for start, ref in zip(starts, down_refs)
        )
        own_ref[:, columns] = partial[:half].astype(jnp.bfloat16)
        other_ref[:, columns] = partial[half:].astype(jnp.bfloat16)
        return carry

    lax.fori_loop(0, own_ref.shape[1] // nb, body, 0)
    for copy in copies:
        copy.wait()


def down(act, weights, part_cols, secs, w_down=None, spans=(), first=0, parts=0):
    tokens, depth = act.shape
    width = weights[0].shape[1]
    vmem = pl.BlockSpec(memory_space=pltpu.VMEM)
    near = [pin(a, pltpu.VMEM) for a in (act, *weights)]
    far = [pin(w_down, pltpu.HBM)] if spans else []
    out_shape = [pltpu.VMEM((tokens // secs, width), jnp.bfloat16)] * secs
    out_shape += [pltpu.VMEM((rows, parts * part_cols), jnp.bfloat16) for _, _, rows in spans]
    return pl.pallas_call(
        functools.partial(
            down_kernel,
            count=len(weights),
            nb=part_cols,
            spans=[span[:2] for span in spans],
            first=first,
            part_cols=part_cols,
        ),
        in_specs=[vmem] * len(near) + [pl.BlockSpec(memory_space=pltpu.HBM)] * len(far),
        out_specs=[vmem] * len(out_shape),
        out_shape=out_shape,
        scratch_shapes=[pltpu.SemaphoreType.DMA((parts,)) for _ in spans],
        cost_estimate=pl.CostEstimate(flops=2 * tokens * depth * width, bytes_accessed=0, transcendentals=0),
        compiler_params=pltpu.CompilerParams(vmem_limit_bytes=4 * MIB),
        name="down",
    )(*near, *far)


def pin(array, space):
    return pltpu.with_memory_space_constraint(array, space)


def swap(array, axis, offset):
    size = lax.axis_size(axis)
    return lax.ppermute(array, axis, [(i, i ^ offset) for i in range(size)])


def on_device(
    resid_in, queries, new_kv, cache, lengths, norm_gain, router, route_ids, w_gate, w_up, w_down
):
    sequences, part_cols = resid_in.shape
    tps, grps, secs = lax.axis_size("tp"), lax.axis_size("grp"), lax.axis_size("sec")
    held = w_gate.shape[0]
    blocks_held = max(1, grps * held // router.shape[1])
    tie = lax.optimization_barrier
    attended, hidden, gain, router_rows, ids = attend(
        lengths, queries, new_kv, resid_in, cache, (norm_gain.reshape(1, -1), router.T, route_ids.T)
    )

    ff = w_down.shape[1]
    late_parts = max(1, tps // 4)
    early_parts = tps - late_parts
    all_spans = [(e, 0, ff) for e in range(held)]
    spans = all_spans[:-1] + [(held - 1, 0, ff // 4), (held - 1, ff // 4, ff - ff // 4)]
    down_jobs = [(w_down, chosen, early_parts, part_cols) for chosen in (spans[:-1], spans[-1:])]
    up_job = (w_up, [(0, 0, w_up.shape[1] // 4)], 0, 0)

    parts = [hidden] + [swap(hidden, "tp", j) for j in range(1, tps)]
    gate_ready, token = fetch(hidden, hidden, [(w_gate, [(0, 0, w_gate.shape[1])], 0, 0)])
    parts, token = tie((parts, token))
    own = norm(gain, router_rows, ids, parts)
    if grps == 4:
        near = [own, swap(own, "grp", 1), swap(own, "grp", 2)]
        *down_ready, up_ready, token = fetch(own, token, [down_jobs[0], up_job])
        near, token = tie((near, token))
        after, right = split(near[2], near[1], tps // 2 * part_cols)
        across = [swap(after, "grp", 1), swap(right, "grp", 2)]
        near = [[array] for array in near]
    else:
        near = [[own]] + [[swap(own, "grp", d)] for d in range(1, grps - 1)]
        after = own
        across = [swap(own, "grp", grps - 1)]
        *down_ready, up_ready, token = fetch(own, token, [down_jobs[0], up_job])
    last_ready, token = fetch(after, token, [down_jobs[1]])
    down_ready.append(last_ready)
    across, token = tie((across, token))
    near.append(across)
    pieces = near + [[swap(array, "sec", 1) for array in arrays] for arrays in near]
    act = gate_up(w_gate, w_up, token, gate_ready, up_ready, pieces, router.shape[1], blocks_held)

    def total(arrays):
        result = arrays[0].astype(jnp.float32)
        for array in arrays[1:]:
            result = result + array.astype(jnp.float32)
        return result

    def send(array, name, offset):
        return swap(array.astype(jnp.bfloat16), name, offset).astype(jnp.float32)

    kept, sent, *down_late = down(act, down_ready, part_cols, secs, w_down, all_spans, early_parts, late_parts)
    early = (kept, swap(sent, "sec", 1))
    act, _ = tie((act, sent))
    kept, sent = down(act, down_late, part_cols, secs)
    late = (kept, swap(sent, "sec", 1))
    sums = [
        [total([array[d * sequences : (d + 1) * sequences] for array in pair]) for pair in (early, late)]
        for d in range(grps)
    ]
    if grps == 4:
        cut = tps // 2 * part_cols
        to_x, to_y = sums[1], sums[2]
        left = send(sums[3][0][:, :cut], "grp", 1)
        right = [send(sums[3][0][:, cut:], "grp", 2), send(sums[3][1], "grp", 2)]
        left, right = tie((left, right))
        to_x = [to_x[0][:, :cut], to_x[0][:, cut:] + right[0], to_x[1] + right[1]]
        to_y = [to_y[0][:, :cut] + left, to_y[0][:, cut:], to_y[1]]
        sums = [sums[0], to_x, to_y]
    sums = [jnp.concatenate(pieces, axis=1) for pieces in sums]
    rows_sum = total([sums[0]] + [send(sums[d], "grp", d) for d in range(1, len(sums))])
    parts = [rows_sum[:, j * part_cols : (j + 1) * part_cols] for j in range(tps)]
    mixed = total([parts[0]] + [send(parts[j], "tp", j) for j in range(1, tps)])
    hidden_part = resid_in.astype(jnp.float32) + attended.astype(jnp.float32)
    return (hidden_part + mixed).astype(jnp.bfloat16)


def solution(mesh):
    return jax.shard_map(
        on_device,
        mesh=mesh,
        in_specs=(
            P(("sec", "grp"), "tp"),
            P(("sec", "grp"), "tp"),
            P(("sec", "grp"), None, "tp"),
            P(("sec", "grp"), None, None, "tp"),
            P(("sec", "grp")),
            P(),
            P(),
            P(("sec", "grp"), None),
            P("grp", None, ("sec", "tp")),
            P("grp", None, ("sec", "tp")),
            P("grp", ("sec", "tp"), None),
        ),
        out_specs=P(("sec", "grp"), "tp"),
        check_vma=False,
    )
```

```python
import functools
import math

import jax
import jax.numpy as jnp
from jax import lax
from jax.experimental import pallas as pl
from jax.experimental.pallas import tpu as pltpu
from jax.sharding import PartitionSpec as P

HEAD_DIM = 128
ROWS_STEP = 8
MIB = 1 << 20
VMEM_GATE_UP = 25

epsilon = 1e-05


def largest_divisor(total, choices):
    return next(c for c in choices if total % c == 0)


def attend_kernel(
    lengths_hbm, query_hbm, new_hbm, resid_hbm, cache_hbm, *rest, extras, kv_local, group
):
    extra_hbm, rest = rest[:extras], rest[extras:]
    (attended_ref, hidden_ref), extra_refs, rest = rest[:2], rest[2 : 2 + extras], rest[2 + extras :]
    lengths_ref, query_ref, new_ref, resid_ref, cache_ref, query_buf, output_buf, *sems = rest
    small_sem, cache_sem, extra_sem = sems
    rows = ROWS_STEP
    blocks = query_ref.shape[0]
    cache_len = cache_ref.shape[2]
    stacked = group * rows
    factor = 1.0 / math.sqrt(HEAD_DIM)

    def cache_copy(b, kind):
        span = pl.ds(b * rows, rows)
        return pltpu.make_async_copy(
            cache_hbm.at[span, kind], cache_ref.at[span, kind], cache_sem.at[kind, b]
        )

    pairs = ((query_hbm, query_ref), (lengths_hbm, lengths_ref), (new_hbm, new_ref), (resid_hbm, resid_ref))
    small = [pltpu.make_async_copy(*pair, small_sem.at[i]) for i, pair in enumerate(pairs)]
    later = [
        pltpu.make_async_copy(*pair, extra_sem.at[i]) for i, pair in enumerate(zip(extra_hbm, extra_refs))
    ]
    for copy in small:
        copy.start()
    for b in range(blocks):
        for kind in range(2):
            cache_copy(b, kind).start()
    for copy in later:
        copy.start()
    small[0].wait()
    for head in range(kv_local):
        for b in range(blocks):
            query_buf[head, b] = jnp.concatenate(
                [
                    query_ref[b, :, pl.ds((head * group + g) * HEAD_DIM, HEAD_DIM)].astype(jnp.float32)
                    for g in range(group)
                ],
                axis=0,
            ).astype(jnp.bfloat16)
    row_of = lax.broadcasted_iota(jnp.int32, (stacked, 1), 0) % rows

    def lanes_of(head):
        return pl.ds(head * HEAD_DIM, HEAD_DIM)

    def block(b, carry):
        span = pl.ds(pl.multiple_of(b * rows, rows), rows)
        length_col = jnp.zeros((stacked, 1), jnp.int32)
        for n in range(rows):
            length_col = jnp.where(row_of == n, lengths_ref[b * rows + n], length_col)
        valid = lax.broadcasted_iota(jnp.int32, (stacked, cache_len), 1) < length_col
        cache_copy(b, 0).wait()
        scores = []
        for head in range(kv_local):
            query = query_buf[head, b]
            total = jnp.zeros((stacked, cache_len), jnp.float32)
            for n in range(rows):
                full = lax.dot_general(
                    query,
                    cache_ref[b * rows + n, 0, :, lanes_of(head)],
                    (((1,), (1,)), ((), ())),
                    preferred_element_type=jnp.float32,
                )
                total = jnp.where(row_of == n, full, total)
            scores.append(jnp.where(valid, total * factor, -jnp.inf))
        chances = []
        for head in range(kv_local):
            new_key = new_ref[span, 0, lanes_of(head)].astype(jnp.float32)
            query = query_buf[head, b].astype(jnp.float32)
            fresh = (
                jnp.sum(query * jnp.concatenate([new_key] * group, axis=0), axis=1, keepdims=True) * factor
            )
            largest = jnp.maximum(jnp.max(scores[head], axis=1, keepdims=True), fresh)
            weights = jnp.exp(scores[head] - largest)
            fresh_weight = jnp.exp(fresh - largest)
            denominator = jnp.sum(weights, axis=1, keepdims=True) + fresh_weight
            probabilities = (weights / denominator).astype(jnp.bfloat16)
            fresh_prob = (fresh_weight / denominator).astype(jnp.bfloat16).astype(jnp.float32)
            chances.append((probabilities, fresh_prob))
        cache_copy(b, 1).wait()
        for head in range(kv_local):
            probabilities, fresh_prob = chances[head]
            new_value = new_ref[span, 1, lanes_of(head)].astype(jnp.float32)
            output = jnp.zeros((stacked, HEAD_DIM), jnp.float32)
            for n in range(rows):
                full = jnp.dot(
                    probabilities,
                    cache_ref[b * rows + n, 1, :, lanes_of(head)],
                    preferred_element_type=jnp.float32,
                )
                output = jnp.where(row_of == n, full, output)
            output_buf[head, b] = output + fresh_prob * jnp.concatenate([new_value] * group, axis=0)
        return carry

    for copy in small[1:]:
        copy.wait()
    lax.fori_loop(0, blocks, block, 0)
    for head in range(kv_local):
        for g in range(group):
            columns = pl.ds((head * group + g) * HEAD_DIM, HEAD_DIM)
            piece = jnp.concatenate(
                [output_buf[head, b, pl.ds(g * rows, rows)] for b in range(blocks)], axis=0
            ).astype(jnp.bfloat16)
            attended_ref[:, columns] = piece
            resid = jnp.concatenate(
                [resid_ref[b, :, columns].astype(jnp.float32) for b in range(blocks)], axis=0
            )
            hidden_ref[:, columns] = (resid + piece.astype(jnp.float32)).astype(jnp.bfloat16)
    for copy in later:
        copy.wait()


def attend(lengths, queries, new_kv, resid_in, cache, extra):
    sequences, part_cols = queries.shape
    cache_len, kv_cols = cache.shape[2:]
    kv_local = kv_cols // HEAD_DIM
    group = part_cols // kv_cols
    blocks = sequences // ROWS_STEP
    stacked = group * ROWS_STEP
    hbm = pl.BlockSpec(memory_space=pltpu.HBM)
    vmem = pl.BlockSpec(memory_space=pltpu.VMEM)
    queries, resid_in = (a.reshape(blocks, ROWS_STEP, part_cols) for a in (queries, resid_in))
    far = [pin(a, pltpu.HBM) for a in (lengths, queries, new_kv, resid_in, cache, *extra)]
    return pl.pallas_call(
        functools.partial(attend_kernel, extras=len(extra), kv_local=kv_local, group=group),
        in_specs=[hbm] * len(far),
        out_specs=[vmem] * (2 + len(extra)),
        out_shape=[pltpu.VMEM((sequences, part_cols), jnp.bfloat16)] * 2
        + [pltpu.VMEM(array.shape, array.dtype) for array in extra],
        scratch_shapes=[
            pltpu.SMEM(lengths.shape, lengths.dtype),
            pltpu.VMEM(queries.shape, queries.dtype),
            pltpu.VMEM(new_kv.shape, new_kv.dtype),
            pltpu.VMEM(resid_in.shape, resid_in.dtype),
            pltpu.VMEM(cache.shape, cache.dtype),
            pltpu.VMEM((kv_local, blocks, stacked, HEAD_DIM), jnp.bfloat16),
            pltpu.VMEM((kv_local, blocks, stacked, HEAD_DIM), jnp.float32),
            pltpu.SemaphoreType.DMA((4,)),
            pltpu.SemaphoreType.DMA((2, blocks)),
            pltpu.SemaphoreType.DMA((len(extra),)),
        ],
        cost_estimate=pl.CostEstimate(
            flops=0, bytes_accessed=2 * cache.size, transcendentals=0
        ),
        compiler_params=pltpu.CompilerParams(vmem_limit_bytes=16 * MIB),
        name="attend",
    )(*far)


def span_copies(source_hbm, targets, sems, spans, first, part_cols):
    tp = lax.axis_index("tp")
    copies = []
    for (e, row), target, sem in zip(spans, targets, sems):
        rows, width = target.shape
        pieces = sem.shape[0]
        for i in range(pieces):
            if part_cols:
                there = pl.ds(pl.multiple_of((first + i ^ tp) * part_cols, 128), part_cols)
                source, here = source_hbm.at[e, pl.ds(row, rows), there], (slice(None), pl.ds(i * part_cols, part_cols))
            else:
                step = rows // pieces
                source, here = source_hbm.at[e, pl.ds(row + i * step, step)], (pl.ds(i * step, step),)
            copies.append(pltpu.make_async_copy(source, target.at[here], sem.at[i]))
    return copies


def fetch_kernel(after_ref, earlier_ref, *rest, jobs):
    sources, rest = rest[: len(jobs)], rest[len(jobs) :]
    count = sum(len(spans) for spans, _ in jobs)
    targets, token_ref, sems = rest[:count], rest[count], rest[count + 1 :]
    copies, at = [], 0
    for source, (spans, part_cols) in zip(sources, jobs):
        here = slice(at, at + len(spans))
        copies += span_copies(source, targets[here], sems[here], spans, 0, part_cols)
        at += len(spans)
    for copy in copies:
        copy.start()
    token_ref[...] = jnp.zeros_like(token_ref)
    for copy in copies:
        copy.wait()


def fetch(after, earlier, jobs):
    shapes, parts_of = [], []
    for weights, spans, parts, part_cols in jobs:
        for _, _, rows in spans:
            shapes.append((rows, parts * part_cols if parts else weights.shape[2]))
            parts_of.append(parts or 4)
    size = sum(math.prod(shape) for shape in shapes)
    return pl.pallas_call(
        functools.partial(
            fetch_kernel,
            jobs=[([span[:2] for span in spans], part_cols) for _, spans, _, part_cols in jobs],
        ),
        in_specs=[pl.BlockSpec(memory_space=pl.ANY)] * 2 + [pl.BlockSpec(memory_space=pltpu.HBM)] * len(jobs),
        out_specs=[pl.BlockSpec(memory_space=pltpu.VMEM)] * (len(shapes) + 1),
        out_shape=[pltpu.VMEM(shape, jnp.bfloat16) for shape in shapes] + [pltpu.VMEM((8, 128), jnp.float32)],
        scratch_shapes=[pltpu.SemaphoreType.DMA((parts,)) for parts in parts_of],
        cost_estimate=pl.CostEstimate(flops=0, bytes_accessed=2 * size, transcendentals=0),
        compiler_params=pltpu.CompilerParams(vmem_limit_bytes=1 * MIB),
        name="fetch",
    )(after, earlier, *(pin(job[0], pltpu.HBM) for job in jobs))


def norm_kernel(gain_ref, router_ref, ids_ref, *rest):
    part_refs, own_ref = rest[:-1], rest[-1]
    tps = len(part_refs)
    rows, part_cols = part_refs[0].shape
    width = tps * part_cols
    experts = router_ref.shape[0]
    tp = lax.axis_index("tp")
    places = [pl.ds(pl.multiple_of((j ^ tp) * part_cols, 128), part_cols) for j in range(tps)]
    raws = [ref[...].astype(jnp.float32) for ref in part_refs]
    squares = sum(jnp.sum(raw * raw, axis=1, keepdims=True) for raw in raws)
    row_scale = lax.rsqrt(squares / width + epsilon)
    logits = jnp.zeros((rows, 2 * experts), jnp.float32)
    for raw, there in zip(raws, places):
        normed = (raw * row_scale * gain_ref[:, there]).astype(jnp.bfloat16)
        own_ref[:, there] = normed
        router = router_ref[:, there]
        high = router.astype(jnp.bfloat16).astype(jnp.float32)
        both = jnp.concatenate([high, router - high], axis=0).astype(jnp.bfloat16)
        logits += lax.dot_general(
            normed, both, (((1,), (1,)), ((), ())), preferred_element_type=jnp.float32
        )
    logits = logits[:, :experts] + logits[:, experts:]
    square = [lax.broadcasted_iota(jnp.int32, (rows, rows), axis) for axis in range(2)]
    identity = jnp.where(square[0] == square[1], 1.0, 0.0)
    ids = lax.dot_general(
        identity, ids_ref[...].astype(jnp.float32), (((1,), (1,)), ((), ())), preferred_element_type=jnp.float32
    ).astype(jnp.int32)
    names = [ids[:, k : k + 1] for k in range(2)]
    lane = lax.broadcasted_iota(jnp.int32, (rows, experts), 1)
    picked = [jnp.sum(jnp.where(lane == name, logits, 0.0), axis=1, keepdims=True) for name in names]
    mixes = [
        1.0 / (1.0 + jnp.exp(picked[1] - picked[0])),
        1.0 / (1.0 + jnp.exp(picked[0] - picked[1])),
    ]
    lane = lax.broadcasted_iota(jnp.int32, (rows, 128), 1)
    share = sum(jnp.where(lane % experts == name, mix, 0.0) for name, mix in zip(names, mixes))
    high = share.astype(jnp.bfloat16).astype(jnp.float32)
    own_ref[:, pl.ds(width, 128)] = jnp.where(lane < experts, high, share - high).astype(jnp.bfloat16)


def norm(gain, router, route_ids, parts):
    rows, part_cols = parts[0].shape
    vmem = pl.BlockSpec(memory_space=pltpu.VMEM)
    near = [pin(a, pltpu.VMEM) for a in (gain, router, route_ids, *parts)]
    return pl.pallas_call(
        norm_kernel,
        in_specs=[vmem] * len(near),
        out_specs=vmem,
        out_shape=pltpu.VMEM((rows, part_cols * len(parts) + 128), jnp.bfloat16),
        compiler_params=pltpu.CompilerParams(vmem_limit_bytes=2 * MIB),
        name="norm",
    )(*near)


def split_kernel(first_ref, second_ref, left_ref, right_ref):
    cut = left_ref.shape[1]
    left_ref[...] = first_ref[:, pl.ds(0, cut)]
    right_ref[...] = second_ref[:, pl.ds(cut, right_ref.shape[1])]


def split(first, second, cut):
    rows, width = first.shape
    vmem = pl.BlockSpec(memory_space=pltpu.VMEM)
    return pl.pallas_call(
        split_kernel,
        in_specs=[vmem] * 2,
        out_specs=[vmem] * 2,
        out_shape=[pltpu.VMEM((rows, cut), first.dtype), pltpu.VMEM((rows, width - cut), first.dtype)],
        compiler_params=pltpu.CompilerParams(vmem_limit_bytes=1 * MIB),
        name="split",
    )(pin(first, pltpu.VMEM), pin(second, pltpu.VMEM))


def gate_up_kernel(gate_hbm, up_hbm, token_ref, gate_ref, up_ref, *rest, layout, experts, blocks_held, depth, nb):
    pieces = sum(layout)
    piece_refs, (act_ref, buf, rows_ref, sem) = rest[:pieces], rest[pieces:]
    held, width, ff = gate_hbm.shape
    ready = 1
    blocks = ff // nb
    deep = buf.shape[1]
    cuts = width // deep
    steps = (2 * held - ready) * blocks * cuts - 1
    grp = lax.axis_index("grp")

    def block_copy(hbm, e, n, i):
        slot = lax.rem(i, depth)
        columns = pl.ds(pl.multiple_of(n * nb, 128), nb)
        there = pl.ds(pl.multiple_of((i + 1) % cuts * deep, 128), deep)
        return pltpu.make_async_copy(hbm.at[e, there, columns], buf.at[slot], sem.at[slot])

    def start(i):
        first = 0
        for e in range(held):
            kinds = (up_hbm,) if e < ready else (gate_hbm, up_hbm)
            for which, hbm in enumerate(kinds):
                inside = (i + 1) // cuts - first
                hit = (inside >= 0) & (inside < len(kinds) * blocks) & (inside % len(kinds) == which)

                @pl.when(hit)
                def _():
                    block_copy(hbm, e, inside // len(kinds), i).start()

            first += len(kinds) * blocks

    def prime(i, carry):
        start(i)
        return carry

    lax.fori_loop(0, min(depth, steps), prime, 0)

    rows_of, first = [], 0
    for parts in layout:
        rows_of.append(piece_refs[first : first + parts])
        first += parts

    def gather(start_column, size):
        found = []
        for refs in rows_of:
            at = start_column
            for ref in refs:
                if at < ref.shape[1]:
                    found.append(ref[:, pl.ds(at, size)].astype(jnp.float32))
                    break
                at -= ref.shape[1]
        return jnp.concatenate(found, axis=0)

    for k in range(width // deep):
        rows_ref[:, pl.ds(k * deep, deep)] = gather(k * deep, deep).astype(jnp.bfloat16)
    shares = gather(width, 128)
    shares = shares[:, :experts] + shares[:, experts : 2 * experts]
    lane = lax.broadcasted_iota(jnp.int32, shares.shape, 1)

    def streamed(block, has_first=False):
        product = 0.0
        for cut in range(cuts):
            there = pl.ds(cut * deep, deep)
            if cut == 0 and has_first:
                product += jnp.dot(rows_ref[:, there], up_ref[...], preferred_element_type=jnp.float32)
                continue
            i = block * cuts + cut - 1
            block_copy(gate_hbm, 0, 0, i).wait()
            product += jnp.dot(
                rows_ref[:, there], buf[lax.rem(i, depth)], preferred_element_type=jnp.float32
            )

            @pl.when(i + depth < steps)
            def _():
                start(i + depth)

        return product

    first = 0
    for e in range(held):
        expert = (grp * held + e) // blocks_held
        share = jnp.sum(jnp.where(lane == expert, shares, 0.0), axis=1, keepdims=True)

        def body(n, carry, e=e, first=first, share=share):
            columns = pl.ds(pl.multiple_of(n * nb, 128), nb)
            if e < ready:
                i = first + n
                gate = jnp.dot(rows_ref[...], gate_ref[:, columns], preferred_element_type=jnp.float32)
            else:
                i = first + 2 * n + 1
                gate = streamed(i - 1)
            up = streamed(i, e < ready) * share
            out = pl.ds(pl.multiple_of(e * ff + n * nb, 128), nb)
            act_ref[:, out] = (gate / (1.0 + jnp.exp(-gate)) * up).astype(jnp.bfloat16)
            return carry

        lax.fori_loop(0, blocks, body, 0)
        first += (1 if e < ready else 2) * blocks


def gate_up(w_gate, w_up, token, gate_ready, up_ready, pieces, experts, blocks_held):
    held, width, ff = w_gate.shape
    tokens = sum(parts[0].shape[0] for parts in pieces)
    nb = largest_divisor(ff, (1024, 512, 256, 128))
    depth, cuts = 5, 4
    vmem = pl.BlockSpec(memory_space=pltpu.VMEM)
    hbm = pl.BlockSpec(memory_space=pltpu.HBM)
    near = [pin(a, pltpu.VMEM) for a in (gate_ready, up_ready, *(part for parts in pieces for part in parts))]
    return pl.pallas_call(
        functools.partial(
            gate_up_kernel,
            layout=tuple(len(parts) for parts in pieces),
            experts=experts,
            blocks_held=blocks_held,
            depth=depth,
            nb=nb,
        ),
        in_specs=[hbm] * 2 + [pl.BlockSpec(memory_space=pl.ANY)] + [vmem] * len(near),
        out_specs=vmem,
        out_shape=pltpu.VMEM((tokens, held * ff), jnp.bfloat16),
        scratch_shapes=[
            pltpu.VMEM((depth, width // cuts, nb), jnp.bfloat16),
            pltpu.VMEM((tokens, width), jnp.bfloat16),
            pltpu.SemaphoreType.DMA((depth,)),
        ],
        cost_estimate=pl.CostEstimate(
            flops=4 * held * tokens * width * ff, bytes_accessed=4 * held * width * ff, transcendentals=0
        ),
        compiler_params=pltpu.CompilerParams(vmem_limit_bytes=VMEM_GATE_UP * MIB),
        name="gate_up",
    )(pin(w_gate, pltpu.HBM), pin(w_up, pltpu.HBM), token, *near)


def down_kernel(act_ref, *rest, count, nb, spans, first, part_cols):
    down_refs, rest = rest[:count], rest[count:]
    if spans:
        down_hbm, own_ref, other_ref, *rest = rest
        targets, sems = rest[: len(spans)], rest[len(spans) :]
        copies = span_copies(down_hbm, targets, sems, spans, first, part_cols)
    else:
        copies, (own_ref, other_ref) = [], rest
    for copy in copies:
        copy.start()
    starts = [sum(ref.shape[0] for ref in down_refs[:i]) for i in range(count)]
    half = own_ref.shape[0]

    def body(i, carry):
        columns = pl.ds(pl.multiple_of(i * nb, 128), nb)
        partial = sum(
            jnp.dot(
                act_ref[:, pl.ds(start, ref.shape[0])], ref[:, columns], preferred_element_type=jnp.float32
            )
            for start, ref in zip(starts, down_refs)
        )
        own_ref[:, columns] = partial[:half].astype(jnp.bfloat16)
        other_ref[:, columns] = partial[half:].astype(jnp.bfloat16)
        return carry

    lax.fori_loop(0, own_ref.shape[1] // nb, body, 0)
    for copy in copies:
        copy.wait()


def down(act, weights, part_cols, secs, w_down=None, spans=(), first=0, parts=0):
    tokens, depth = act.shape
    width = weights[0].shape[1]
    vmem = pl.BlockSpec(memory_space=pltpu.VMEM)
    near = [pin(a, pltpu.VMEM) for a in (act, *weights)]
    far = [pin(w_down, pltpu.HBM)] if spans else []
    out_shape = [pltpu.VMEM((tokens // secs, width), jnp.bfloat16)] * secs
    out_shape += [pltpu.VMEM((rows, parts * part_cols), jnp.bfloat16) for _, _, rows in spans]
    return pl.pallas_call(
        functools.partial(
            down_kernel,
            count=len(weights),
            nb=part_cols,
            spans=[span[:2] for span in spans],
            first=first,
            part_cols=part_cols,
        ),
        in_specs=[vmem] * len(near) + [pl.BlockSpec(memory_space=pltpu.HBM)] * len(far),
        out_specs=[vmem] * len(out_shape),
        out_shape=out_shape,
        scratch_shapes=[pltpu.SemaphoreType.DMA((parts,)) for _ in spans],
        cost_estimate=pl.CostEstimate(flops=2 * tokens * depth * width, bytes_accessed=0, transcendentals=0),
        compiler_params=pltpu.CompilerParams(vmem_limit_bytes=4 * MIB),
        name="down",
    )(*near, *far)


def pin(array, space):
    return pltpu.with_memory_space_constraint(array, space)


def swap(array, axis, offset):
    size = lax.axis_size(axis)
    return lax.ppermute(array, axis, [(i, i ^ offset) for i in range(size)])


def on_device(
    resid_in, queries, new_kv, cache, lengths, norm_gain, router, route_ids, w_gate, w_up, w_down
):
    sequences, part_cols = resid_in.shape
    tps, grps, secs = lax.axis_size("tp"), lax.axis_size("grp"), lax.axis_size("sec")
    held = w_gate.shape[0]
    blocks_held = max(1, grps * held // router.shape[1])
    tie = lax.optimization_barrier
    attended, hidden, gain, router_rows, ids = attend(
        lengths, queries, new_kv, resid_in, cache, (norm_gain.reshape(1, -1), router.T, route_ids.T)
    )

    ff = w_down.shape[1]
    late_parts = max(1, tps // 4)
    early_parts = tps - late_parts
    all_spans = [(e, 0, ff) for e in range(held)]
    spans = all_spans[:-1] + [(held - 1, 0, ff // 4), (held - 1, ff // 4, ff - ff // 4)]
    down_jobs = [(w_down, chosen, early_parts, part_cols) for chosen in (spans[:-1], spans[-1:])]
    up_job = (w_up, [(0, 0, w_up.shape[1] // 4)], 0, 0)

    parts = [hidden] + [swap(hidden, "tp", j) for j in range(1, tps)]
    gate_ready, token = fetch(hidden, hidden, [(w_gate, [(0, 0, w_gate.shape[1])], 0, 0)])
    parts, token = tie((parts, token))
    own = norm(gain, router_rows, ids, parts)
    if grps == 4:
        near = [own, swap(own, "grp", 1), swap(own, "grp", 2)]
        *down_ready, up_ready, token = fetch(own, token, [down_jobs[0], up_job])
        near, token = tie((near, token))
        after, right = split(near[2], near[1], tps // 2 * part_cols)
        across = [swap(after, "grp", 1), swap(right, "grp", 2)]
        near = [[array] for array in near]
    else:
        near = [[own]] + [[swap(own, "grp", d)] for d in range(1, grps - 1)]
        after = own
        across = [swap(own, "grp", grps - 1)]
        *down_ready, up_ready, token = fetch(own, token, [down_jobs[0], up_job])
    last_ready, token = fetch(after, token, [down_jobs[1]])
    down_ready.append(last_ready)
    across, token = tie((across, token))
    near.append(across)
    pieces = near + [[swap(array, "sec", 1) for array in arrays] for arrays in near]
    act = gate_up(w_gate, w_up, token, gate_ready, up_ready, pieces, router.shape[1], blocks_held)

    def total(arrays):
        result = arrays[0].astype(jnp.float32)
        for array in arrays[1:]:
            result = result + array.astype(jnp.float32)
        return result

    def send(array, name, offset):
        return swap(array.astype(jnp.bfloat16), name, offset).astype(jnp.float32)

    kept, sent, *down_late = down(act, down_ready, part_cols, secs, w_down, all_spans, early_parts, late_parts)
    early = (kept, swap(sent, "sec", 1))
    act, _ = tie((act, sent))
    kept, sent = down(act, down_late, part_cols, secs)
    late = (kept, swap(sent, "sec", 1))
    sums = [
        [total([array[d * sequences : (d + 1) * sequences] for array in pair]) for pair in (early, late)]
        for d in range(grps)
    ]
    if grps == 4:
        cut = tps // 2 * part_cols
        to_x, to_y = sums[1], sums[2]
        left = send(sums[3][0][:, :cut], "grp", 1)
        right = [send(sums[3][0][:, cut:], "grp", 2), send(sums[3][1], "grp", 2)]
        left, right = tie((left, right))
        to_x = [to_x[0][:, :cut], to_x[0][:, cut:] + right[0], to_x[1] + right[1]]
        to_y = [to_y[0][:, :cut] + left, to_y[0][:, cut:], to_y[1]]
        sums = [sums[0], to_x, to_y]
    sums = [jnp.concatenate(pieces, axis=1) for pieces in sums]
    rows_sum = total([sums[0]] + [send(sums[d], "grp", d) for d in range(1, len(sums))])
    parts = [rows_sum[:, j * part_cols : (j + 1) * part_cols] for j in range(tps)]
    mixed = total([parts[0]] + [send(parts[j], "tp", j) for j in range(1, tps)])
    hidden_part = resid_in.astype(jnp.float32) + attended.astype(jnp.float32)
    return (hidden_part + mixed).astype(jnp.bfloat16)


def solution(mesh):
    return jax.shard_map(
        on_device,
        mesh=mesh,
        in_specs=(
            P(("sec", "grp"), "tp"),
            P(("sec", "grp"), "tp"),
            P(("sec", "grp"), None, "tp"),
            P(("sec", "grp"), None, None, "tp"),
            P(("sec", "grp")),
            P(),
            P(),
            P(("sec", "grp"), None),
            P("grp", None, ("sec", "tp")),
            P("grp", None, ("sec", "tp")),
            P("grp", ("sec", "tp"), None),
        ),
        out_specs=P(("sec", "grp"), "tp"),
        check_vma=False,
    )
```

```python
import functools
import math

import jax
import jax.numpy as jnp
from jax import lax
from jax.experimental import pallas as pl
from jax.experimental.pallas import tpu as pltpu
from jax.sharding import PartitionSpec as P

HEAD_DIM = 128
ROWS_STEP = 8
MIB = 1 << 20
VMEM_GATE_UP = 25

epsilon = 1e-05


def largest_divisor(total, choices):
    return next(c for c in choices if total % c == 0)


def attend_kernel(
    lengths_hbm, query_hbm, new_hbm, resid_hbm, cache_hbm, *rest, extras, kv_local, group
):
    extra_hbm, rest = rest[:extras], rest[extras:]
    (whole_ref, hidden_ref), extra_refs, rest = rest[:2], rest[2 : 2 + extras], rest[2 + extras :]
    lengths_ref, query_ref, new_ref, resid_ref, cache_ref, query_buf, output_buf, *sems = rest
    small_sem, cache_sem, extra_sem = sems
    rows = ROWS_STEP
    blocks = query_ref.shape[0]
    cache_len = cache_ref.shape[2]
    stacked = group * rows
    factor = 1.0 / math.sqrt(HEAD_DIM)

    def cache_copy(b, kind):
        span = pl.ds(b * rows, rows)
        return pltpu.make_async_copy(
            cache_hbm.at[span, kind], cache_ref.at[span, kind], cache_sem.at[kind, b]
        )

    pairs = ((query_hbm, query_ref), (lengths_hbm, lengths_ref), (new_hbm, new_ref), (resid_hbm, resid_ref))
    small = [pltpu.make_async_copy(*pair, small_sem.at[i]) for i, pair in enumerate(pairs)]
    later = [
        pltpu.make_async_copy(*pair, extra_sem.at[i]) for i, pair in enumerate(zip(extra_hbm, extra_refs))
    ]
    for copy in small:
        copy.start()
    for b in range(blocks):
        for kind in range(2):
            cache_copy(b, kind).start()
    for copy in later:
        copy.start()
    small[0].wait()
    for head in range(kv_local):
        for b in range(blocks):
            query_buf[head, b] = jnp.concatenate(
                [
                    query_ref[b, :, pl.ds((head * group + g) * HEAD_DIM, HEAD_DIM)].astype(jnp.float32)
                    for g in range(group)
                ],
                axis=0,
            ).astype(jnp.bfloat16)
    row_of = lax.broadcasted_iota(jnp.int32, (stacked, 1), 0) % rows

    def lanes_of(head):
        return pl.ds(head * HEAD_DIM, HEAD_DIM)

    def block(b, carry):
        span = pl.ds(pl.multiple_of(b * rows, rows), rows)
        length_col = jnp.zeros((stacked, 1), jnp.int32)
        for n in range(rows):
            length_col = jnp.where(row_of == n, lengths_ref[b * rows + n], length_col)
        valid = lax.broadcasted_iota(jnp.int32, (stacked, cache_len), 1) < length_col
        cache_copy(b, 0).wait()
        scores = []
        for head in range(kv_local):
            query = query_buf[head, b]
            total = jnp.zeros((stacked, cache_len), jnp.float32)
            for n in range(rows):
                full = lax.dot_general(
                    query,
                    cache_ref[b * rows + n, 0, :, lanes_of(head)],
                    (((1,), (1,)), ((), ())),
                    preferred_element_type=jnp.float32,
                )
                total = jnp.where(row_of == n, full, total)
            scores.append(jnp.where(valid, total * factor, -jnp.inf))
        chances = []
        for head in range(kv_local):
            new_key = new_ref[span, 0, lanes_of(head)].astype(jnp.float32)
            query = query_buf[head, b].astype(jnp.float32)
            fresh = (
                jnp.sum(query * jnp.concatenate([new_key] * group, axis=0), axis=1, keepdims=True) * factor
            )
            largest = jnp.maximum(jnp.max(scores[head], axis=1, keepdims=True), fresh)
            weights = jnp.exp(scores[head] - largest)
            fresh_weight = jnp.exp(fresh - largest)
            denominator = jnp.sum(weights, axis=1, keepdims=True) + fresh_weight
            probabilities = (weights / denominator).astype(jnp.bfloat16)
            fresh_prob = (fresh_weight / denominator).astype(jnp.bfloat16).astype(jnp.float32)
            chances.append((probabilities, fresh_prob))
        cache_copy(b, 1).wait()
        for head in range(kv_local):
            probabilities, fresh_prob = chances[head]
            new_value = new_ref[span, 1, lanes_of(head)].astype(jnp.float32)
            output = jnp.zeros((stacked, HEAD_DIM), jnp.float32)
            for n in range(rows):
                full = jnp.dot(
                    probabilities,
                    cache_ref[b * rows + n, 1, :, lanes_of(head)],
                    preferred_element_type=jnp.float32,
                )
                output = jnp.where(row_of == n, full, output)
            output_buf[head, b] = output + fresh_prob * jnp.concatenate([new_value] * group, axis=0)
        return carry

    for copy in small[1:]:
        copy.wait()
    lax.fori_loop(0, blocks, block, 0)
    for head in range(kv_local):
        for g in range(group):
            columns = pl.ds((head * group + g) * HEAD_DIM, HEAD_DIM)
            piece = jnp.concatenate(
                [output_buf[head, b, pl.ds(g * rows, rows)] for b in range(blocks)], axis=0
            ).astype(jnp.bfloat16)
            resid = jnp.concatenate(
                [resid_ref[b, :, columns].astype(jnp.float32) for b in range(blocks)], axis=0
            )
            hidden = resid + piece.astype(jnp.float32)
            whole_ref[:, columns] = hidden
            hidden_ref[:, columns] = hidden.astype(jnp.bfloat16)
    for copy in later:
        copy.wait()


def attend(lengths, queries, new_kv, resid_in, cache, extra):
    sequences, part_cols = queries.shape
    cache_len, kv_cols = cache.shape[2:]
    kv_local = kv_cols // HEAD_DIM
    group = part_cols // kv_cols
    blocks = sequences // ROWS_STEP
    stacked = group * ROWS_STEP
    hbm = pl.BlockSpec(memory_space=pltpu.HBM)
    vmem = pl.BlockSpec(memory_space=pltpu.VMEM)
    queries, resid_in = (a.reshape(blocks, ROWS_STEP, part_cols) for a in (queries, resid_in))
    far = [pin(a, pltpu.HBM) for a in (lengths, queries, new_kv, resid_in, cache, *extra)]
    return pl.pallas_call(
        functools.partial(attend_kernel, extras=len(extra), kv_local=kv_local, group=group),
        in_specs=[hbm] * len(far),
        out_specs=[vmem] * (2 + len(extra)),
        out_shape=[pltpu.VMEM((sequences, part_cols), dtype) for dtype in (jnp.float32, jnp.bfloat16)]
        + [pltpu.VMEM(array.shape, array.dtype) for array in extra],
        scratch_shapes=[
            pltpu.SMEM(lengths.shape, lengths.dtype),
            pltpu.VMEM(queries.shape, queries.dtype),
            pltpu.VMEM(new_kv.shape, new_kv.dtype),
            pltpu.VMEM(resid_in.shape, resid_in.dtype),
            pltpu.VMEM(cache.shape, cache.dtype),
            pltpu.VMEM((kv_local, blocks, stacked, HEAD_DIM), jnp.bfloat16),
            pltpu.VMEM((kv_local, blocks, stacked, HEAD_DIM), jnp.float32),
            pltpu.SemaphoreType.DMA((4,)),
            pltpu.SemaphoreType.DMA((2, blocks)),
            pltpu.SemaphoreType.DMA((len(extra),)),
        ],
        cost_estimate=pl.CostEstimate(
            flops=0, bytes_accessed=2 * cache.size, transcendentals=0
        ),
        compiler_params=pltpu.CompilerParams(vmem_limit_bytes=16 * MIB),
        name="attend",
    )(*far)


def span_copies(source_hbm, targets, sems, spans, first, part_cols):
    tp = lax.axis_index("tp")
    copies = []
    for (e, row), target, sem in zip(spans, targets, sems):
        rows, width = target.shape
        pieces = sem.shape[0]
        for i in range(pieces):
            if part_cols:
                there = pl.ds(pl.multiple_of((first + i ^ tp) * part_cols, 128), part_cols)
                source, here = source_hbm.at[e, pl.ds(row, rows), there], (slice(None), pl.ds(i * part_cols, part_cols))
            else:
                step = rows // pieces
                source, here = source_hbm.at[e, pl.ds(row + i * step, step)], (pl.ds(i * step, step),)
            copies.append(pltpu.make_async_copy(source, target.at[here], sem.at[i]))
    return copies


def fetch_kernel(after_ref, earlier_ref, *rest, jobs):
    sources, rest = rest[: len(jobs)], rest[len(jobs) :]
    count = sum(len(spans) for spans, _ in jobs)
    targets, token_ref, sems = rest[:count], rest[count], rest[count + 1 :]
    copies, at = [], 0
    for source, (spans, part_cols) in zip(sources, jobs):
        here = slice(at, at + len(spans))
        copies += span_copies(source, targets[here], sems[here], spans, 0, part_cols)
        at += len(spans)
    for copy in copies:
        copy.start()
    token_ref[...] = jnp.zeros_like(token_ref)
    for copy in copies:
        copy.wait()


def fetch(after, earlier, jobs):
    shapes, parts_of = [], []
    for weights, spans, parts, part_cols in jobs:
        for _, _, rows in spans:
            shapes.append((rows, parts * part_cols if parts else weights.shape[2]))
            parts_of.append(parts or 4)
    size = sum(math.prod(shape) for shape in shapes)
    return pl.pallas_call(
        functools.partial(
            fetch_kernel,
            jobs=[([span[:2] for span in spans], part_cols) for _, spans, _, part_cols in jobs],
        ),
        in_specs=[pl.BlockSpec(memory_space=pl.ANY)] * 2 + [pl.BlockSpec(memory_space=pltpu.HBM)] * len(jobs),
        out_specs=[pl.BlockSpec(memory_space=pltpu.VMEM)] * (len(shapes) + 1),
        out_shape=[pltpu.VMEM(shape, jnp.bfloat16) for shape in shapes] + [pltpu.VMEM((8, 128), jnp.float32)],
        scratch_shapes=[pltpu.SemaphoreType.DMA((parts,)) for parts in parts_of],
        cost_estimate=pl.CostEstimate(flops=0, bytes_accessed=2 * size, transcendentals=0),
        compiler_params=pltpu.CompilerParams(vmem_limit_bytes=1 * MIB),
        name="fetch",
    )(after, earlier, *(pin(job[0], pltpu.HBM) for job in jobs))


def norm_kernel(gain_ref, router_ref, ids_ref, *rest):
    part_refs, own_ref = rest[:-1], rest[-1]
    tps = len(part_refs)
    rows, part_cols = part_refs[0].shape
    width = tps * part_cols
    experts = router_ref.shape[0]
    tp = lax.axis_index("tp")
    places = [pl.ds(pl.multiple_of((j ^ tp) * part_cols, 128), part_cols) for j in range(tps)]
    raws = [ref[...].astype(jnp.float32) for ref in part_refs]
    squares = sum(jnp.sum(raw * raw, axis=1, keepdims=True) for raw in raws)
    row_scale = lax.rsqrt(squares / width + epsilon)
    logits = jnp.zeros((rows, 2 * experts), jnp.float32)
    for raw, there in zip(raws, places):
        normed = (raw * row_scale * gain_ref[:, there]).astype(jnp.bfloat16)
        own_ref[:, there] = normed
        router = router_ref[:, there]
        high = router.astype(jnp.bfloat16).astype(jnp.float32)
        both = jnp.concatenate([high, router - high], axis=0).astype(jnp.bfloat16)
        logits += lax.dot_general(
            normed, both, (((1,), (1,)), ((), ())), preferred_element_type=jnp.float32
        )
    logits = logits[:, :experts] + logits[:, experts:]
    square = [lax.broadcasted_iota(jnp.int32, (rows, rows), axis) for axis in range(2)]
    identity = jnp.where(square[0] == square[1], 1.0, 0.0)
    ids = lax.dot_general(
        identity, ids_ref[...].astype(jnp.float32), (((1,), (1,)), ((), ())), preferred_element_type=jnp.float32
    ).astype(jnp.int32)
    names = [ids[:, k : k + 1] for k in range(2)]
    lane = lax.broadcasted_iota(jnp.int32, (rows, experts), 1)
    picked = [jnp.sum(jnp.where(lane == name, logits, 0.0), axis=1, keepdims=True) for name in names]
    mixes = [
        1.0 / (1.0 + jnp.exp(picked[1] - picked[0])),
        1.0 / (1.0 + jnp.exp(picked[0] - picked[1])),
    ]
    lane = lax.broadcasted_iota(jnp.int32, (rows, 128), 1)
    share = sum(jnp.where(lane % experts == name, mix, 0.0) for name, mix in zip(names, mixes))
    high = share.astype(jnp.bfloat16).astype(jnp.float32)
    own_ref[:, pl.ds(width, 128)] = jnp.where(lane < experts, high, share - high).astype(jnp.bfloat16)


def norm(gain, router, route_ids, parts):
    rows, part_cols = parts[0].shape
    vmem = pl.BlockSpec(memory_space=pltpu.VMEM)
    near = [pin(a, pltpu.VMEM) for a in (gain, router, route_ids, *parts)]
    return pl.pallas_call(
        norm_kernel,
        in_specs=[vmem] * len(near),
        out_specs=vmem,
        out_shape=pltpu.VMEM((rows, part_cols * len(parts) + 128), jnp.bfloat16),
        compiler_params=pltpu.CompilerParams(vmem_limit_bytes=2 * MIB),
        name="norm",
    )(*near)


def split_kernel(first_ref, second_ref, left_ref, right_ref):
    cut = left_ref.shape[1]
    left_ref[...] = first_ref[:, pl.ds(0, cut)]
    right_ref[...] = second_ref[:, pl.ds(cut, right_ref.shape[1])]


def split(first, second, cut):
    rows, width = first.shape
    vmem = pl.BlockSpec(memory_space=pltpu.VMEM)
    return pl.pallas_call(
        split_kernel,
        in_specs=[vmem] * 2,
        out_specs=[vmem] * 2,
        out_shape=[pltpu.VMEM((rows, cut), first.dtype), pltpu.VMEM((rows, width - cut), first.dtype)],
        compiler_params=pltpu.CompilerParams(vmem_limit_bytes=1 * MIB),
        name="split",
    )(pin(first, pltpu.VMEM), pin(second, pltpu.VMEM))


def gate_up_kernel(gate_hbm, up_hbm, token_ref, gate_ref, up_ref, *rest, layout, experts, blocks_held, depth, nb):
    pieces = sum(layout)
    piece_refs, (act_ref, buf, rows_ref, early_ref, sem) = rest[:pieces], rest[pieces:]
    held, width, ff = gate_hbm.shape
    ready = 1
    blocks = ff // nb
    deep = buf.shape[1]
    cuts = width // deep
    steps = (2 * held - ready) * blocks * cuts - 1
    grp = lax.axis_index("grp")

    def block_copy(hbm, e, n, i):
        slot = lax.rem(i, depth)
        columns = pl.ds(pl.multiple_of(n * nb, 128), nb)
        there = pl.ds(pl.multiple_of((i + 1) % cuts * deep, 128), deep)
        return pltpu.make_async_copy(hbm.at[e, there, columns], buf.at[slot], sem.at[slot])

    def start(i):
        first = 0
        for e in range(held):
            kinds = (up_hbm,) if e < ready else (gate_hbm, up_hbm)
            for which, hbm in enumerate(kinds):
                inside = (i + 1) // cuts - first
                hit = (inside >= 0) & (inside < len(kinds) * blocks) & (inside % len(kinds) == which)

                @pl.when(hit)
                def _():
                    block_copy(hbm, e, inside // len(kinds), i).start()

            first += len(kinds) * blocks

    def prime(i, carry):
        start(i)
        return carry

    lax.fori_loop(0, min(depth, steps), prime, 0)

    rows_of, first = [], 0
    for parts in layout:
        rows_of.append(piece_refs[first : first + parts])
        first += parts

    def gather(start_column, size):
        found = []
        for refs in rows_of:
            at = start_column
            for ref in refs:
                if at < ref.shape[1]:
                    found.append(ref[:, pl.ds(at, size)].astype(jnp.float32))
                    break
                at -= ref.shape[1]
        return jnp.concatenate(found, axis=0)

    early = 0.0
    for k in range(width // deep):
        value = gather(k * deep, deep).astype(jnp.bfloat16)
        rows_ref[:, pl.ds(k * deep, deep)] = value
        early += jnp.dot(value, gate_ref[pl.ds(k * deep, deep), :], preferred_element_type=jnp.float32)
    early_ref[...] = early
    shares = gather(width, 128)
    shares = shares[:, :experts] + shares[:, experts : 2 * experts]
    lane = lax.broadcasted_iota(jnp.int32, shares.shape, 1)

    def streamed(block, has_first=False):
        product = 0.0
        for cut in range(cuts):
            there = pl.ds(cut * deep, deep)
            if cut == 0 and has_first:
                product += jnp.dot(rows_ref[:, there], up_ref[...], preferred_element_type=jnp.float32)
                continue
            i = block * cuts + cut - 1
            block_copy(gate_hbm, 0, 0, i).wait()
            product += jnp.dot(
                rows_ref[:, there], buf[lax.rem(i, depth)], preferred_element_type=jnp.float32
            )

            @pl.when(i + depth < steps)
            def _():
                start(i + depth)

        return product

    first = 0
    for e in range(held):
        expert = (grp * held + e) // blocks_held
        share = jnp.sum(jnp.where(lane == expert, shares, 0.0), axis=1, keepdims=True)

        def body(n, carry, e=e, first=first, share=share):
            columns = pl.ds(pl.multiple_of(n * nb, 128), nb)
            if e < ready:
                i = first + n
                gate = early_ref[:, columns]
            else:
                i = first + 2 * n + 1
                gate = streamed(i - 1)
            up = streamed(i, e < ready) * share
            out = pl.ds(pl.multiple_of(e * ff + n * nb, 128), nb)
            act_ref[:, out] = (gate / (1.0 + jnp.exp(-gate)) * up).astype(jnp.bfloat16)
            return carry

        lax.fori_loop(0, blocks, body, 0)
        first += (1 if e < ready else 2) * blocks


def gate_up(w_gate, w_up, token, gate_ready, up_ready, pieces, experts, blocks_held):
    held, width, ff = w_gate.shape
    tokens = sum(parts[0].shape[0] for parts in pieces)
    nb = largest_divisor(ff, (1024, 512, 256, 128))
    depth, cuts = 5, 4
    vmem = pl.BlockSpec(memory_space=pltpu.VMEM)
    hbm = pl.BlockSpec(memory_space=pltpu.HBM)
    near = [pin(a, pltpu.VMEM) for a in (gate_ready, up_ready, *(part for parts in pieces for part in parts))]
    return pl.pallas_call(
        functools.partial(
            gate_up_kernel,
            layout=tuple(len(parts) for parts in pieces),
            experts=experts,
            blocks_held=blocks_held,
            depth=depth,
            nb=nb,
        ),
        in_specs=[hbm] * 2 + [pl.BlockSpec(memory_space=pl.ANY)] + [vmem] * len(near),
        out_specs=vmem,
        out_shape=pltpu.VMEM((tokens, held * ff), jnp.bfloat16),
        scratch_shapes=[
            pltpu.VMEM((depth, width // cuts, nb), jnp.bfloat16),
            pltpu.VMEM((tokens, width), jnp.bfloat16),
            pltpu.VMEM((tokens, ff), jnp.float32),
            pltpu.SemaphoreType.DMA((depth,)),
        ],
        cost_estimate=pl.CostEstimate(
            flops=4 * held * tokens * width * ff, bytes_accessed=4 * held * width * ff, transcendentals=0
        ),
        compiler_params=pltpu.CompilerParams(vmem_limit_bytes=VMEM_GATE_UP * MIB),
        name="gate_up",
    )(pin(w_gate, pltpu.HBM), pin(w_up, pltpu.HBM), token, *near)


def down_kernel(act_ref, *rest, count, nb, spans, first, part_cols):
    down_refs, rest = rest[:count], rest[count:]
    if spans:
        down_hbm, own_ref, other_ref, *rest = rest
        targets, sems = rest[: len(spans)], rest[len(spans) :]
        copies = span_copies(down_hbm, targets, sems, spans, first, part_cols)
    else:
        copies, (own_ref, other_ref) = [], rest
    for copy in copies:
        copy.start()
    starts = [sum(ref.shape[0] for ref in down_refs[:i]) for i in range(count)]
    half = own_ref.shape[0]

    def body(i, carry):
        columns = pl.ds(pl.multiple_of(i * nb, 128), nb)
        partial = sum(
            jnp.dot(
                act_ref[:, pl.ds(start, ref.shape[0])], ref[:, columns], preferred_element_type=jnp.float32
            )
            for start, ref in zip(starts, down_refs)
        )
        own_ref[:, columns] = partial[:half].astype(jnp.bfloat16)
        other_ref[:, columns] = partial[half:].astype(jnp.bfloat16)
        return carry

    lax.fori_loop(0, own_ref.shape[1] // nb, body, 0)
    for copy in copies:
        copy.wait()


def down(act, weights, part_cols, secs, w_down=None, spans=(), first=0, parts=0):
    tokens, depth = act.shape
    width = weights[0].shape[1]
    vmem = pl.BlockSpec(memory_space=pltpu.VMEM)
    near = [pin(a, pltpu.VMEM) for a in (act, *weights)]
    far = [pin(w_down, pltpu.HBM)] if spans else []
    out_shape = [pltpu.VMEM((tokens // secs, width), jnp.bfloat16)] * secs
    out_shape += [pltpu.VMEM((rows, parts * part_cols), jnp.bfloat16) for _, _, rows in spans]
    return pl.pallas_call(
        functools.partial(
            down_kernel,
            count=len(weights),
            nb=part_cols,
            spans=[span[:2] for span in spans],
            first=first,
            part_cols=part_cols,
        ),
        in_specs=[vmem] * len(near) + [pl.BlockSpec(memory_space=pltpu.HBM)] * len(far),
        out_specs=[vmem] * len(out_shape),
        out_shape=out_shape,
        scratch_shapes=[pltpu.SemaphoreType.DMA((parts,)) for _ in spans],
        cost_estimate=pl.CostEstimate(flops=2 * tokens * depth * width, bytes_accessed=0, transcendentals=0),
        compiler_params=pltpu.CompilerParams(vmem_limit_bytes=4 * MIB),
        name="down",
    )(*near, *far)


def pin(array, space):
    return pltpu.with_memory_space_constraint(array, space)


def swap(array, axis, offset):
    size = lax.axis_size(axis)
    return lax.ppermute(array, axis, [(i, i ^ offset) for i in range(size)])


def on_device(
    resid_in, queries, new_kv, cache, lengths, norm_gain, router, route_ids, w_gate, w_up, w_down
):
    sequences, part_cols = resid_in.shape
    tps, grps, secs = lax.axis_size("tp"), lax.axis_size("grp"), lax.axis_size("sec")
    held = w_gate.shape[0]
    blocks_held = max(1, grps * held // router.shape[1])
    tie = lax.optimization_barrier
    hidden_part, hidden, gain, router_rows, ids = attend(
        lengths, queries, new_kv, resid_in, cache, (norm_gain.reshape(1, -1), router.T, route_ids.T)
    )

    ff = w_down.shape[1]
    late_parts = max(1, tps // 4)
    early_parts = tps - late_parts
    all_spans = [(e, 0, ff) for e in range(held)]
    spans = all_spans[:-1] + [(held - 1, 0, ff // 4), (held - 1, ff // 4, ff - ff // 4)]
    down_jobs = [(w_down, chosen, early_parts, part_cols) for chosen in (spans[:-1], spans[-1:])]
    up_job = (w_up, [(0, 0, w_up.shape[1] // 4)], 0, 0)

    parts = [hidden] + [swap(hidden, "tp", j) for j in range(1, tps)]
    gate_ready, token = fetch(hidden, hidden, [(w_gate, [(0, 0, w_gate.shape[1])], 0, 0)])
    parts, token = tie((parts, token))
    own = norm(gain, router_rows, ids, parts)
    if grps == 4:
        near = [own, swap(own, "grp", 1), swap(own, "grp", 2)]
        *down_ready, up_ready, token = fetch(own, token, [down_jobs[0], up_job])
        near, token = tie((near, token))
        after, right = split(near[2], near[1], tps // 2 * part_cols)
        across = [swap(after, "grp", 1), swap(right, "grp", 2)]
        near = [[array] for array in near]
    else:
        near = [[own]] + [[swap(own, "grp", d)] for d in range(1, grps - 1)]
        after = own
        across = [swap(own, "grp", grps - 1)]
        *down_ready, up_ready, token = fetch(own, token, [down_jobs[0], up_job])
    last_ready, token = fetch(after, token, [down_jobs[1]])
    down_ready.append(last_ready)
    across, token = tie((across, token))
    near.append(across)
    pieces = near + [[swap(array, "sec", 1) for array in arrays] for arrays in near]
    act = gate_up(w_gate, w_up, token, gate_ready, up_ready, pieces, router.shape[1], blocks_held)

    def total(arrays):
        result = arrays[0].astype(jnp.float32)
        for array in arrays[1:]:
            result = result + array.astype(jnp.float32)
        return result

    def send(array, name, offset):
        return swap(array.astype(jnp.bfloat16), name, offset).astype(jnp.float32)

    kept, sent, *down_late = down(act, down_ready, part_cols, secs, w_down, all_spans, early_parts, late_parts)
    early = (kept, swap(sent, "sec", 1))
    act, _ = tie((act, sent))
    kept, sent = down(act, down_late, part_cols, secs)
    late = (kept, swap(sent, "sec", 1))
    sums = [
        [total([array[d * sequences : (d + 1) * sequences] for array in pair]) for pair in (early, late)]
        for d in range(grps)
    ]
    if grps == 4:
        cut = tps // 2 * part_cols
        to_x, to_y = sums[1], sums[2]
        left = send(sums[3][0][:, :cut], "grp", 1)
        right = [send(sums[3][0][:, cut:], "grp", 2), send(sums[3][1], "grp", 2)]
        left, right = tie((left, right))
        to_x = [to_x[0][:, :cut], to_x[0][:, cut:] + right[0], to_x[1] + right[1]]
        to_y = [to_y[0][:, :cut] + left, to_y[0][:, cut:], to_y[1]]
        sums = [sums[0], to_x, to_y]
    sums = [jnp.concatenate(pieces, axis=1) for pieces in sums]
    rows_sum = total([sums[0]] + [send(sums[d], "grp", d) for d in range(1, len(sums))])
    parts = [rows_sum[:, j * part_cols : (j + 1) * part_cols] for j in range(tps)]
    mixed = total([parts[0]] + [send(parts[j], "tp", j) for j in range(1, tps)])
    return (hidden_part + mixed).astype(jnp.bfloat16)


def solution(mesh):
    return jax.shard_map(
        on_device,
        mesh=mesh,
        in_specs=(
            P(("sec", "grp"), "tp"),
            P(("sec", "grp"), "tp"),
            P(("sec", "grp"), None, "tp"),
            P(("sec", "grp"), None, None, "tp"),
            P(("sec", "grp")),
            P(),
            P(),
            P(("sec", "grp"), None),
            P("grp", None, ("sec", "tp")),
            P("grp", None, ("sec", "tp")),
            P("grp", ("sec", "tp"), None),
        ),
        out_specs=P(("sec", "grp"), "tp"),
        check_vma=False,
    )
```
